32 devices in a mesh: gz: 8 (over y, x, core), xy: 4 (over z).
Axes of the slice: x: 2, y: 2, z: 4, core: 2. Of those that a mesh axis runs over, the one named last changes fastest.
Arguments:
- prior_estimate: float32 [384, 128, 128], P('gz', 'xy'), may hold values from 0.5 to 2
- views_upright: float32 [3, 384, 128, 128], P(None, 'gz', 'xy'), may hold values from 0.2 to 5
- views_turned: float32 [3, 384, 128, 128], P(None, 'gz', 'xy'), may hold values from 0.2 to 5
- kernel_depth: float32 [6, 61], replicated, may hold values from 0.005 to 1.55, as said below
- kernel_rows: float32 [6, 31], replicated, may hold values from 0.005 to 1.55, as said below
- kernel_columns: float32 [6, 31], replicated, may hold values from 0.005 to 1.55, as said below
- lateral_offsets: int32 [6], replicated, may hold values from -8 to 8, as said below
- block_views: int32 [32, 3], replicated, may hold values from 0 to 5, all different within a row
Outputs:
- estimate: float32 [384, 128, 128], P('gz', 'xy')
The draws below stay inside these ranges and needn't reach their ends.
Inputs may be any that keep to these rules, and one draw needn't show every extreme that they name: `block_views`: row r holds 3 different views and belongs to the block at position r // 4 along gz and r % 4 along xy. `lateral_offsets`: one view has offset 8 and another -8. `kernel_depth`: positive taps. `kernel_rows`: positive taps. `kernel_columns`: positive taps.
All inputs are finite; a program needn't handle non-finite values.
Results may differ from the reference program's by a relative error of at most 0.00005.
Values sent between devices are 32-bit elements; how exact they have to be, the bound alone decides.
No kernel may reach another device: no remote copies, remote signals or barrier semaphores. Data moves between devices by JAX's collectives and lax.ppermute only.
A program may use at most 128 MiB of HBM per device.

```python
import math
import jax
import jax.numpy as jnp
from jax import lax

CZ = 48
CY = 32
VIEWS = 6
ACTIVE = 3
HZ = 61
HY = 31
HX = 31
OFF = 8
ITERS = 2
HALF = 3
NZ = 384
NY = 128
NX = 128
NBLOCKS = 32
N_GZ = 8
N_XY = 4


def draw_lateral_offsets(key, part):
    value_key = jax.random.fold_in(key, 11)
    perm_key = jax.random.fold_in(key, 23)
    values = jax.random.randint(value_key, (VIEWS,), -OFF, OFF + 1, dtype=jnp.int32)
    ranking = jax.random.permutation(perm_key, VIEWS)
    values = values.at[ranking[0]].set(OFF)
    values = values.at[ranking[1]].set(-OFF)
    return values


def tap_profile(key, extent, width_low, width_high, ripple_low, ripple_high):
    radius = (extent - 1) // 2
    width_key = jax.random.fold_in(key, 3)
    base_key = jax.random.fold_in(key, 5)
    ripple_key = jax.random.fold_in(key, 7)
    breadth = jnp.exp(jax.random.uniform(width_key, (VIEWS, 1), jnp.float32, jnp.log(width_low), jnp.log(width_high)))
    places = jnp.arange(extent, dtype=jnp.float32)[None, :] - radius
    profile = jnp.exp(-0.5 * (places / breadth) ** 2)
    baseline = jax.random.uniform(base_key, (VIEWS, 1), jnp.float32, 0.01, 0.03)
    ripple = jax.random.uniform(ripple_key, (VIEWS, extent), jnp.float32, ripple_low, ripple_high)
    return ((profile + baseline) * ripple).astype(jnp.float32)


def draw_kernel_depth(key, part):
    inner_key = jax.random.fold_in(key, 101)
    return tap_profile(inner_key, HZ, 3.0, 6.0, 0.6, 1.4)


def draw_kernel_rows(key, part):
    inner_key = jax.random.fold_in(key, 202)
    return tap_profile(inner_key, HY, 1.0, 2.0, 0.6, 1.4)


def draw_kernel_columns(key, part):
    inner_key = jax.random.fold_in(key, 303)
    return tap_profile(inner_key, HX, 1.0, 2.0, 0.6, 1.4)


def levels(rng, shape, cuts, smallest, top_value):
    def one(dim, parts):
        heights = jax.random.uniform(jax.random.fold_in(jax.random.fold_in(rng, 6), dim), (parts,), jnp.float32, smallest / len(cuts), top_value / len(cuts))
        return jnp.repeat(jnp.exp(heights), shape[dim] // parts).reshape((-1,) + (1,) * (len(shape) - dim - 1))

    loudness = one(*cuts[0])
    for cut in cuts[1:]:
        loudness = loudness * one(*cut)
    return loudness


def distinct(own_key, rows, number_of, top, lift):
    sequence = jax.random.permutation(jax.random.fold_in(own_key, 1), number_of)
    favour = sequence
    for power in range(3):
        favour = favour * favour // number_of
    favour = favour * lift // number_of
    tickets = jax.random.randint(jax.random.fold_in(own_key, 2), (rows, number_of), 0, 4096) + favour
    holders = jax.random.permutation(jax.random.fold_in(own_key, 3), rows)[jnp.arange(number_of) % rows]
    tickets = jnp.where(jnp.arange(rows)[:, None] == holders[None, :], 1 << 14, tickets)
    priority = tickets * number_of + jnp.arange(number_of)
    return lax.top_k(priority.astype(jnp.int32), top)[1].astype(jnp.int32)


def setup_inputs(seed: int = 0) -> dict:
    key_of = jax.random.split(jax.random.key(seed), 9)
    return {
        "prior_estimate": jnp.clip(jnp.exp(math.log(2.0) - 1.3862944 * jax.random.uniform(key_of[0], (NZ, NY, NX), jnp.float32) ** levels(key_of[0], (NZ, NY, NX), ((0, 8), (1, 4)), -0.2, 0.2)), 0.5, 2.0),
        "views_upright": jnp.clip(jnp.exp(math.log(5.0) - 3.218876 * jax.random.uniform(key_of[1], (HALF, NZ, NY, NX), jnp.float32) ** levels(key_of[1], (HALF, NZ, NY, NX), ((1, 8), (2, 4)), -0.2, 0.2)), 0.2, 5.0),
        "views_turned": jnp.clip(jnp.exp(math.log(5.0) - 3.218876 * jax.random.uniform(key_of[2], (HALF, NZ, NX, NY), jnp.float32) ** levels(key_of[2], (HALF, NZ, NX, NY), ((1, 8), (2, 4)), -0.2, 0.2)), 0.2, 5.0),
        "kernel_depth": draw_kernel_depth(jax.random.fold_in(key_of[8], 71), 0),
        "kernel_rows": draw_kernel_rows(jax.random.fold_in(key_of[8], 71), 0),
        "kernel_columns": draw_kernel_columns(jax.random.fold_in(key_of[8], 71), 0),
        "lateral_offsets": draw_lateral_offsets(jax.random.fold_in(key_of[8], 71), 0),
        "block_views": distinct(key_of[7], NBLOCKS, VIEWS, ACTIVE, 4096),
    }


def normalize(kernel):
    return kernel / jnp.sum(kernel, axis=-1, keepdims=True)


def axis_pass(volume, kernel, axis, reverse):
    extent = kernel.shape[0]
    radius = (extent - 1) // 2
    length = volume.shape[axis]
    padding = [(0, 0), (0, 0), (0, 0)]
    padding[axis] = (radius, radius)
    padded = jnp.pad(volume, padding)
    summed = jnp.zeros_like(volume)
    for tap_index in range(extent):
        anchor = 2 * radius - tap_index if reverse else tap_index
        summed = summed + kernel[tap_index] * lax.slice_in_dim(padded, anchor, anchor + length, axis=2 if axis == 2 else axis)
    return summed


def lateral_pass(volume, kernel, displacement, reverse):
    extent = kernel.shape[0]
    radius = (extent - 1) // 2
    margin = radius + OFF
    length = volume.shape[2]
    padded = jnp.pad(volume, ((0, 0), (0, 0), (margin, margin)))
    summed = jnp.zeros_like(volume)
    for tap_index in range(extent):
        if reverse:
            anchor = 2 * radius + OFF + displacement - tap_index
        else:
            anchor = OFF + tap_index - displacement
        window = lax.dynamic_slice_in_dim(padded, anchor.astype(jnp.int32), length, 2)
        summed = summed + kernel[tap_index] * window
    return summed


def reference(prior_estimate, views_upright, views_turned, kernel_depth, kernel_rows, kernel_columns, lateral_offsets, block_views):
    taps_depth = normalize(kernel_depth)
    taps_rows = normalize(kernel_rows)
    taps_columns = normalize(kernel_columns)
    turned = jnp.transpose(views_turned, (0, 1, 3, 2))
    observed = jnp.concatenate([views_upright, turned], axis=0)
    member = jnp.sum((block_views[:, :, None] == jnp.arange(VIEWS, dtype=jnp.int32)[None, None, :]).astype(jnp.float32), axis=1) / ACTIVE
    layout = member.reshape(N_GZ, N_XY, VIEWS)
    weight_field = jnp.repeat(jnp.repeat(layout, CZ, axis=0), CY, axis=1)
    estimate = prior_estimate
    for iteration in range(ITERS):
        correction = jnp.zeros_like(estimate)
        for view_index in range(VIEWS):
            blurred = axis_pass(estimate, taps_depth[view_index], 0, False)
            blurred = axis_pass(blurred, taps_rows[view_index], 1, False)
            blurred = lateral_pass(blurred, taps_columns[view_index], lateral_offsets[view_index], False)
            quotient = observed[view_index] / blurred
            back = axis_pass(quotient, taps_depth[view_index], 0, True)
            back = axis_pass(back, taps_rows[view_index], 1, True)
            back = lateral_pass(back, taps_columns[view_index], lateral_offsets[view_index], True)
            correction = correction + weight_field[:, :, view_index][:, :, None] * back
        estimate = estimate * correction
    return estimate
```

```python
import functools

import jax
import jax.numpy as jnp
from jax import lax
from jax.experimental import pallas as pl
from jax.experimental.pallas import tpu as pltpu
from jax.sharding import PartitionSpec as P

ITERS = 2
F32 = jnp.float32
BF16 = jnp.bfloat16
VMEM_LIMIT = 60 * 1024 * 1024


def round_up(value, unit):
    return -(-value // unit) * unit


def shifted(value, axis, step):
    count = lax.axis_size(axis)
    if step > 0:
        pairs = [(i, i + 1) for i in range(count - 1)]
    else:
        pairs = [(i + 1, i) for i in range(count - 1)]
    return lax.ppermute(value, axis, pairs)


def top_part(value):
    return lax.reduce_precision(value, 8, 7)


def split_cols(matrix):
    high = top_part(matrix)
    low = matrix - high
    return jnp.concatenate([high, high, low], axis=-1).astype(BF16)


def split_square(matrix):
    high = top_part(matrix)
    low = matrix - high
    upper = jnp.concatenate([high, low], axis=-1)
    lower = jnp.concatenate([high, jnp.zeros_like(low)], axis=-1)
    return jnp.concatenate([upper, lower], axis=-2).astype(BF16)


def halves(value):
    high = value.astype(BF16)
    low = (value - high.astype(F32)).astype(BF16)
    return high, low


def banded(taps, index):
    extent = taps.shape[-1]
    pick = index[..., None] == jnp.arange(extent, dtype=jnp.int32)
    return jnp.sum(jnp.where(pick, taps[:, None, None, :], 0.0), axis=-1)


def forward_kernel(sizes, c, clo, chi, s, slo, shi, wz, wy, wx, out, mid):
    depth, rows, reach, zpad, views = sizes
    width = c.shape[-1]
    side = s.shape[0] // depth
    total = rows + side
    step = pl.program_id(0)

    @pl.when(step == 0)
    def _():
        fill = jnp.zeros((zpad - reach, width), F32)

        def column(low, centre, high, y, n):
            return jnp.concatenate(
                [
                    low[pl.ds(y, reach, stride=n), :],
                    fill,
                    centre[pl.ds(y, depth, stride=n), :],
                    high[pl.ds(y, reach, stride=n), :],
                    fill,
                ],
                axis=0,
            )

        def run(low, centre, high, n, base):
            def body(i, carry):
                both = jnp.concatenate(
                    [column(low, centre, high, 2 * i + j, n) for j in range(2)], axis=1
                )
                top, rest = halves(both)
                data = jnp.concatenate([top, rest, top], axis=0)
                result = jnp.dot(wz[...], data, preferred_element_type=F32)
                for j in range(2):
                    mid[pl.ds(base + 2 * i + j, views * depth, stride=total), :] = result[
                        :, j * width : (j + 1) * width
                    ]
                return carry

            lax.fori_loop(0, n // 2, body, 0)

        run(clo, c, chi, rows, 0)
        run(slo, s, shi, side, rows)

    @pl.when(step > 0)
    def _():
        view = step - 1
        group = 8

        def body(i, carry):
            start = (view * depth + i * group) * total
            lines = []
            for j in range(group // 2):
                at = pl.multiple_of(start + 2 * j * total, total)
                both = jnp.concatenate(
                    [mid[pl.ds(at, total), :], mid[pl.ds(at + total, total), :]], axis=1
                )
                top, rest = halves(both)
                data = jnp.concatenate([top, rest, top], axis=0)
                result = jnp.dot(wy[0], data, preferred_element_type=F32)
                lines += [result[:, :width], result[:, width:]]
            flat = jnp.concatenate(lines, axis=0)
            top, rest = halves(flat)
            result = jnp.dot(
                jnp.concatenate([top, rest], axis=1), wx[0], preferred_element_type=F32
            )
            at = pl.multiple_of(i * (group * rows), group * rows)
            out[0, pl.ds(at, group * rows), :] = result[:, :width] + result[:, width:]
            return carry

        lax.fori_loop(0, depth // group, body, 0)


def forward(sizes, c, clo, chi, s, slo, shi, wz, wy, wx):
    depth, rows, reach, zpad, views = sizes
    width = c.shape[-1]
    side = s.shape[0] // depth
    total = rows + side
    whole = lambda a: pl.BlockSpec(a.shape, lambda i: (0,) * a.ndim)
    per_view = lambda a: pl.BlockSpec(
        (1,) + a.shape[1:], lambda i: (jnp.maximum(i - 1, 0),) + (0,) * (a.ndim - 1)
    )
    result = jax.ShapeDtypeStruct((views, depth * rows, width), F32)
    return pl.pallas_call(
        functools.partial(forward_kernel, sizes),
        out_shape=result,
        grid=(views + 1,),
        in_specs=[whole(a) for a in (c, clo, chi, s, slo, shi, wz)] + [per_view(wy), per_view(wx)],
        out_specs=per_view(result),
        scratch_shapes=[pltpu.VMEM((views * depth * total, width), F32)],
        compiler_params=pltpu.CompilerParams(vmem_limit_bytes=VMEM_LIMIT),
        cost_estimate=pl.CostEstimate(
            flops=6 * 10**9, bytes_accessed=12 * 10**6, transcendentals=0
        ),
        name="forward",
    )(c, clo, chi, s, slo, shi, wz, wy, wx)


def backward_kernel(sizes, side, obs, blur, wx, wy, wzc, wzs, cc, clo, chi, sc, slo, shi, mid):
    depth, rows, reach, zpad, views = sizes
    width = obs.shape[-1]
    total = rows + side
    lines = views * depth
    step = pl.program_id(0)

    @pl.when(step < views)
    def _():
        group = 8

        def body(i, carry):
            at = pl.multiple_of(i * (group * rows), group * rows)
            ratio = obs[0, pl.ds(at, group * rows), :] / blur[0, pl.ds(at, group * rows), :]
            top, rest = halves(ratio)
            flat = jnp.dot(jnp.concatenate([top, rest], axis=1), wx[0], preferred_element_type=F32)
            flat = flat[:, :width] + flat[:, width:]
            for j in range(group // 2):
                both = jnp.concatenate(
                    [
                        flat[2 * j * rows : (2 * j + 1) * rows],
                        flat[(2 * j + 1) * rows : (2 * j + 2) * rows],
                    ],
                    axis=1,
                )
                top, rest = halves(both)
                data = jnp.concatenate([top, rest, top], axis=0)
                result = jnp.dot(wy[0], data, preferred_element_type=F32)
                for k in range(2):
                    line = step * depth + i * group + 2 * j + k
                    mid[pl.ds(line, total, stride=lines), :] = result[
                        :, k * width : (k + 1) * width
                    ]
            return carry

        lax.fori_loop(0, depth // group, body, 0)

    @pl.when(step == views)
    def _():
        def run(weights, low, centre, high, n, base, first, last):
            def body(i, carry):
                at = pl.multiple_of((base + 2 * i) * lines, lines)
                both = jnp.concatenate(
                    [mid[pl.ds(at, lines), :], mid[pl.ds(at + lines, lines), :]], axis=1
                )
                top, rest = halves(both)
                data = jnp.concatenate([top, rest, top], axis=0)
                result = jnp.dot(weights, data, preferred_element_type=F32)
                for j in range(2):
                    part = result[:, j * width : (j + 1) * width]
                    y = 2 * i + j
                    low[pl.ds(y, reach, stride=n), :] = part[:reach]
                    centre[pl.ds(y, depth, stride=n), :] = part[zpad : zpad + depth]
                    high[pl.ds(y, reach, stride=n), :] = part[zpad + depth : zpad + depth + reach]
                return carry

            lax.fori_loop(first, last, body, 0)

        run(wzc[...], clo, cc, chi, rows, 0, 0, rows // 2)
        run(wzs[0], slo, sc, shi, side, rows, 0, side // 4)
        run(wzs[1], slo, sc, shi, side, rows, side // 4, side // 2)


def backward(sizes, side, obs, blur, wx, wy, wzc, wzs):
    depth, rows, reach, zpad, views = sizes
    width = obs.shape[-1]
    total = rows + side
    whole = lambda a: pl.BlockSpec(a.shape, lambda i: (0,) * len(a.shape))
    per_view = lambda a: pl.BlockSpec(
        (1,) + a.shape[1:], lambda i: (jnp.minimum(i, views - 1),) + (0,) * (a.ndim - 1)
    )
    shapes = [
        jax.ShapeDtypeStruct((count * n, width), F32)
        for n in (rows, side)
        for count in (depth, reach, reach)
    ]
    return pl.pallas_call(
        functools.partial(backward_kernel, sizes, side),
        out_shape=shapes,
        grid=(views + 1,),
        in_specs=[per_view(a) for a in (obs, blur, wx, wy)] + [whole(wzc), whole(wzs)],
        out_specs=[whole(a) for a in shapes],
        scratch_shapes=[pltpu.VMEM((total * views * depth, width), F32)],
        compiler_params=pltpu.CompilerParams(vmem_limit_bytes=VMEM_LIMIT),
        cost_estimate=pl.CostEstimate(
            flops=6 * 10**9, bytes_accessed=12 * 10**6, transcendentals=0
        ),
        name="backward",
    )(obs, blur, wx, wy, wzc, wzs)


def pack_kernel(count, per, x, out):
    rows = x.shape[-1] // count
    for g in range(x.shape[0] // per):
        for d in range(count):
            out[d, g] = jnp.concatenate(
                [x[g * per + j, :, d * rows : (d + 1) * rows] for j in range(per)], axis=1
            )


def pack(turned, count, per):
    planes, xl, yf = turned.shape
    block = 48 if planes % 48 == 0 else per
    return pl.pallas_call(
        functools.partial(pack_kernel, count, per),
        out_shape=jax.ShapeDtypeStruct((count, planes // per, xl, per * (yf // count)), F32),
        grid=(planes // block,),
        in_specs=[pl.BlockSpec((block, xl, yf), lambda i: (i, 0, 0))],
        out_specs=pl.BlockSpec(
            (count, block // per, xl, per * (yf // count)), lambda i: (0, i, 0, 0)
        ),
        compiler_params=pltpu.CompilerParams(vmem_limit_bytes=VMEM_LIMIT),
        name="pack",
    )(turned)


def unpack_kernel(x, out):
    for g in range(x.shape[1]):
        stacked = jnp.concatenate([x[k, g] for k in range(x.shape[0])], axis=0)
        out[g] = stacked.T


def unpack(received):
    count, groups, xl, lanes = received.shape
    block = 12 if groups % 12 == 0 else 1
    return pl.pallas_call(
        unpack_kernel,
        out_shape=jax.ShapeDtypeStruct((groups, lanes, count * xl), F32),
        grid=(groups // block,),
        in_specs=[pl.BlockSpec((count, block, xl, lanes), lambda i: (0, i, 0, 0))],
        out_specs=pl.BlockSpec((block, lanes, count * xl), lambda i: (i, 0, 0)),
        compiler_params=pltpu.CompilerParams(vmem_limit_bytes=VMEM_LIMIT),
        name="unpack",
    )(received)


def normalize(kernel):
    return kernel / jnp.sum(kernel, axis=-1, keepdims=True)


def local(
    prior_estimate,
    views_upright,
    views_turned,
    kernel_depth,
    kernel_rows,
    kernel_columns,
    lateral_offsets,
    block_views,
):
    depth, rows, width = prior_estimate.shape
    views = kernel_depth.shape[0]
    reach = (kernel_depth.shape[1] - 1) // 2
    reach_y = (kernel_rows.shape[1] - 1) // 2
    reach_x = (kernel_columns.shape[1] - 1) // 2
    zpad = round_up(reach, 16)
    ypad = round_up(reach_y, 8)
    side = 2 * ypad
    sizes = (depth, rows, reach, zpad, views)
    n_xy = lax.axis_size("xy")
    n_gz = lax.axis_size("gz")

    half = views_turned.shape[0]
    per = width // rows
    packed = pack(
        views_turned.reshape(half * depth, views_turned.shape[2], views_turned.shape[3]), n_xy, per
    )
    received = lax.all_to_all(packed, "xy", split_axis=0, concat_axis=0, tiled=True)
    turned = unpack(received).reshape(half, depth * rows, width)
    observed = jnp.concatenate(
        [views_upright.reshape(views - half, depth * rows, width), turned], axis=0
    )

    taps_z = normalize(kernel_depth)
    taps_y = normalize(kernel_rows)
    taps_x = normalize(kernel_columns)
    z_in = jnp.arange(depth, dtype=jnp.int32)
    low = jnp.arange(zpad, dtype=jnp.int32)
    far = jnp.int32(1 << 20)
    z_ext = jnp.concatenate(
        [
            jnp.where(low < reach, low - reach, far),
            z_in,
            jnp.where(low < reach, low + depth, far),
        ]
    )
    y_in = jnp.arange(rows, dtype=jnp.int32)
    rim = jnp.arange(ypad, dtype=jnp.int32)
    y_ext = jnp.concatenate([y_in, rim - ypad, rim + rows])
    x_in = jnp.arange(width, dtype=jnp.int32)
    band_z = banded(taps_z, (z_ext[None, :] - z_in[:, None] + reach)[None])
    band_y = banded(taps_y, (y_ext[None, :] - y_in[:, None] + reach_y)[None])
    band_x = banded(
        taps_x,
        (x_in[None, :] - x_in[:, None] + reach_x)[None] + lateral_offsets[:, None, None],
    )
    wz_f = split_cols(band_z.reshape(views * depth, z_ext.shape[0]))
    wy_f = split_cols(band_y)
    wx_f = split_square(jnp.swapaxes(band_x, 1, 2))
    wx_b = split_square(band_x)
    wy_b = split_cols(jnp.swapaxes(band_y, 1, 2))

    member = jnp.sum(
        (block_views[:, :, None] == jnp.arange(views, dtype=jnp.int32)).astype(F32), axis=1
    ) / block_views.shape[1]
    member = member.reshape(n_gz, n_xy, views)
    near = jnp.arange(3, dtype=jnp.int32) - 1
    near_z = jnp.clip(lax.axis_index("gz") + near, 0, n_gz - 1)
    near_y = jnp.clip(lax.axis_index("xy") + near, 0, n_xy - 1)
    pick_z = (near_z[:, None] == jnp.arange(n_gz, dtype=jnp.int32)).astype(F32)
    pick_y = (near_y[:, None] == jnp.arange(n_xy, dtype=jnp.int32)).astype(F32)
    around = jnp.sum(pick_z[:, :, None, None] * member, axis=1)
    around = jnp.sum(pick_y[None, :, :, None] * around[:, None], axis=2)
    by_row = jnp.concatenate(
        [
            jnp.broadcast_to(around[i][None], (n,) + around.shape[1:])
            for i, n in enumerate((zpad, depth, zpad))
        ]
    )
    spread = jnp.transpose(band_z, (2, 0, 1))
    wz_b = [
        split_cols((spread * by_row[:, b, :, None]).reshape(z_ext.shape[0], views * depth))
        for b in range(3)
    ]
    wz_centre = wz_b[1]
    wz_side = jnp.stack([wz_b[0], wz_b[2]])

    estimate = prior_estimate
    for iteration in range(ITERS):
        from_left = shifted(estimate[:, rows - ypad :], "xy", 1)
        from_right = shifted(estimate[:, :ypad], "xy", -1)
        below = shifted(estimate[depth - reach :], "gz", 1)
        above = shifted(estimate[:reach], "gz", -1)
        sides = jnp.concatenate([from_left, from_right], axis=1)
        side_below = shifted(sides[depth - reach :], "gz", 1)
        side_above = shifted(sides[:reach], "gz", -1)
        flat = lambda a: a.reshape(-1, width)
        blurred = forward(
            sizes,
            *(flat(a) for a in (estimate, below, above, sides, side_below, side_above)),
            wz_f,
            wy_f,
            wx_f,
        )
        cc, clo, chi, sc, slo, shi = backward(
            sizes, side, observed, blurred, wx_b, wy_b, wz_centre, wz_side
        )
        cube = lambda a, n: a.reshape(-1, n, width)
        cc, clo, chi = (cube(a, rows) for a in (cc, clo, chi))
        sc, slo, shi = (cube(a, side) for a in (sc, slo, shi))
        s_low = shifted(shi, "gz", 1)
        s_high = shifted(slo, "gz", -1)
        c_low = shifted(chi, "gz", 1)
        c_high = shifted(clo, "gz", -1)
        head = ((0, depth - reach), (0, 0), (0, 0))
        tail = ((depth - reach, 0), (0, 0), (0, 0))
        sc = sc + jnp.pad(s_low, head) + jnp.pad(s_high, tail)
        from_left = shifted(sc[:, ypad:], "xy", 1)
        from_right = shifted(sc[:, :ypad], "xy", -1)
        cc = cc + jnp.pad(c_low, head) + jnp.pad(c_high, tail)
        cc = cc + jnp.pad(from_left, ((0, 0), (0, rows - ypad), (0, 0)))
        cc = cc + jnp.pad(from_right, ((0, 0), (rows - ypad, 0), (0, 0)))
        estimate = estimate * cc
    return estimate


def solution(mesh):
    in_specs = (
        P("gz", "xy", None),
        P(None, "gz", "xy", None),
        P(None, "gz", "xy", None),
        P(),
        P(),
        P(),
        P(),
        P(),
    )
    out_specs = P("gz", "xy", None)
    return jax.shard_map(local, mesh=mesh, in_specs=in_specs, out_specs=out_specs, check_vma=False)
```

```python
import functools

import jax
import jax.numpy as jnp
from jax import lax
from jax.experimental import pallas as pl
from jax.experimental.pallas import tpu as pltpu
from jax.sharding import PartitionSpec as P

ITERS = 2
F32 = jnp.float32
BF16 = jnp.bfloat16
VMEM_LIMIT = 36 * 1024 * 1024


def round_up(value, unit):
    return -(-value // unit) * unit


def exchange(low, high, axis):
    count = lax.axis_size(axis)
    even = lax.axis_index(axis) % 2 == 0
    rounds = [
        [pair for i in range(begin, count - 1, 2) for pair in ((i, i + 1), (i + 1, i))]
        for begin in (0, 1)
    ]
    a = lax.ppermute(jnp.where(even, high, low), axis, rounds[0])
    b = lax.ppermute(jnp.where(even, low, high), axis, rounds[1])
    return jnp.where(even, b, a), jnp.where(even, a, b)


def halves(value):
    high = value.astype(BF16)
    low = (value - high.astype(F32)).astype(BF16)
    return high, low


def stack(value):
    top, rest = halves(value)
    return jnp.concatenate([top, rest, top], axis=0)


def update_kernel(plan, *refs):
    refs = list(refs)
    take = lambda n: [refs.pop(0) for _ in range(n)]
    depth, rows, side, reach, zpad = plan.depth, plan.rows, plan.side, plan.reach, plan.zpad
    width = plan.width
    total = rows + side
    pitch_y = total + 2
    if plan.forward:
        c, clo, chi, s, slo, shi, wzf, wyf, wxf = take(9)
    if plan.upright_back:
        obs_u, wzb_u = take(2)
    if plan.turned_back:
        obs_t, wzb_t = take(2)
        if not plan.forward:
            (blur_in,) = take(1)
            acc = take(6)
    wxb, wyb = take(2)
    if plan.turned_back:
        outs = take(6)
    else:
        outs = take(6)
        (blur_out,) = take(1)
    if plan.forward:
        (mid,) = take(1)
    (back,) = take(1)
    copies = []
    if plan.turned_back and not plan.forward:
        held = take(6)
        (arrived,) = take(1)
        copies = [
            pltpu.make_async_copy(x, y, arrived.at[i]) for i, (x, y) in enumerate(zip(acc, held))
        ]
        acc = held

        @pl.when(pl.program_id(0) == 0)
        def _():
            for copy in copies:
                copy.start()

    step = pl.program_id(0)
    first = 1 if plan.forward else 0
    n_up = plan.upright if (plan.forward) else 0
    n_all = n_up + plan.turned
    lines = plan.lines
    pitch_z = lines + 8
    group = plan.group

    if plan.forward:

        @pl.when(step == 0)
        def _():
            fill = jnp.zeros((zpad - reach, width), F32)

            def column(low, centre, high, y, n):
                return jnp.concatenate(
                    [
                        low[pl.ds(y, reach, stride=n), :],
                        fill,
                        centre[pl.ds(y, depth, stride=n), :],
                        high[pl.ds(y, reach, stride=n), :],
                        fill,
                    ],
                    axis=0,
                )

            def run(low, centre, high, n, base):
                def body(i, carry):
                    both = jnp.concatenate(
                        [column(low, centre, high, 2 * i + j, n) for j in range(2)], axis=1
                    )
                    result = jnp.dot(wzf[...], stack(both), preferred_element_type=F32)
                    for j in range(2):
                        mid[pl.ds(base + 2 * i + j, n_all * depth, stride=pitch_y), :] = result[
                            :, j * width : (j + 1) * width
                        ]
                    return carry

                lax.fori_loop(0, n // 2, body, 0, unroll=8)

            run(clo, c, chi, rows, 0)
            run(slo, s, shi, side, rows)

    def blur_lines(view, i):
        start = (view * depth + i * group) * pitch_y
        pieces = []
        for j in range(group // 2):
            at = start + 2 * j * pitch_y
            both = jnp.concatenate(
                [mid[pl.ds(at, total), :], mid[pl.ds(at + pitch_y, total), :]], axis=1
            )
            top, rest = halves(both)
            result = jnp.dot(
                wyf[0], jnp.concatenate([top, rest], axis=0), preferred_element_type=F32
            )
            result = result[:rows] + result[rows:]
            pieces += [result[:, :width], result[:, width:]]
        top, rest = halves(jnp.concatenate(pieces, axis=0))
        result = jnp.dot(
            jnp.concatenate([top, rest], axis=1), wxf[0], preferred_element_type=F32
        )
        return result[:, :width] + result[:, width:]

    def spread_lines(slot, i, ratio):
        top, rest = halves(ratio)
        flat = jnp.dot(jnp.concatenate([top, rest], axis=1), wxb[0], preferred_element_type=F32)
        flat = flat[:, :width] + flat[:, width:]
        for j in range(group // 2):
            both = jnp.concatenate(
                [flat[(2 * j + k) * rows : (2 * j + k + 1) * rows] for k in range(2)], axis=1
            )
            result = jnp.dot(wyb[0], stack(both), preferred_element_type=F32)
            for k in range(2):
                line = slot * depth + i * group + 2 * j + k
                back[pl.ds(line, total, stride=pitch_z), :] = result[
                    :, k * width : (k + 1) * width
                ]

    def turned_lines(i):
        per = plan.per
        blocks = []
        for g in range(group // per):
            at = i * (group // per) + g
            blocks.append(jnp.concatenate([obs_t[k, at] for k in range(plan.count)], axis=0).T)
        return jnp.concatenate(blocks, axis=0)

    size = group * rows
    window = lambda i: pl.ds(pl.multiple_of(i * size, size), size)

    def loop(body):
        def wrapped(i, carry):
            body(i)
            return carry

        lax.fori_loop(0, depth // group, wrapped, 0, unroll=plan.unroll)

    if plan.upright_back:

        @pl.when((step >= first) & (step < first + n_up))
        def _():
            view = step - first

            def body(i):
                spread_lines(view, i, obs_u[0, window(i), :] / blur_lines(view, i))

            loop(body)

    @pl.when((step >= first + n_up) & (step < first + n_all))
    def _():
        view = step - first

        def body(i):
            blurred = blur_lines(view, i) if plan.forward else blur_in[0, window(i), :]
            if plan.turned_back:
                spread_lines(view, i, turned_lines(i) / blurred)
            else:
                blur_out[0, window(i), :] = blurred

        loop(body)

    @pl.when(step == first + n_all)
    def _():
        for copy in copies:
            copy.wait()
        banks = []
        if plan.upright_back:
            banks.append((wzb_u, 0, plan.upright * depth))
        if plan.turned_back:
            banks.append((wzb_t, n_up * depth, plan.turned * depth))

        def run(region, targets, adds, n, base, begin, end):
            def body(i, carry):
                at = (base + 2 * i) * pitch_z
                result = None
                for weights, offset, count in banks:
                    both = jnp.concatenate(
                        [back[pl.ds(at + j * pitch_z + offset, count), :] for j in range(2)],
                        axis=1,
                    )
                    term = jnp.dot(weights[region], stack(both), preferred_element_type=F32)
                    result = term if result is None else result + term
                for j in range(2):
                    part = result[:, j * width : (j + 1) * width]
                    for target, add, low, count in zip(
                        targets, adds, (zpad, 0, zpad + depth), (depth, reach, reach)
                    ):
                        spot = (pl.ds(2 * i + j, count, stride=n), slice(None))
                        piece = part[low : low + count]
                        if add is not None:
                            piece = piece + add[spot]
                        target[spot] = piece
                return carry

            lax.fori_loop(begin, end, body, 0, unroll=4)

        adds = acc if (plan.turned_back and not plan.forward) else [None] * 6
        run(0, outs[3:], adds[3:], side, rows, 0, side // 4)
        run(2, outs[3:], adds[3:], side, rows, side // 4, side // 2)
        run(1, outs[:3], adds[:3], rows, 0, 0, rows // 2)


class Plan:
    def __init__(self, **fields):
        self.__dict__.update(fields)


def update(plan, **a):
    first = 1 if plan.forward else 0
    n_up = plan.upright if plan.forward else 0
    n_all = n_up + plan.turned
    used = (plan.upright if plan.upright_back else 0) + (plan.turned if plan.turned_back else 0)
    plan.lines = used * plan.depth
    total = plan.rows + plan.side
    shift = plan.upright - n_up
    once = pl.Buffered(1)

    def whole(x):
        return pl.BlockSpec(x.shape, lambda i: (0,) * len(x.shape), pipeline_mode=once)

    def per_view(x, start, count, offset=0):
        return pl.BlockSpec(
            (1,) + x.shape[1:],
            lambda i: (jnp.clip(i - start, 0, count - 1) + offset,) + (0,) * (len(x.shape) - 1),
        )

    args, specs = [], []

    def give(x, spec):
        args.append(x)
        specs.append(spec)

    if plan.forward:
        for x in a["volumes"]:
            give(x, whole(x))
        give(a["wzf"], whole(a["wzf"]))
        give(a["wyf"], per_view(a["wyf"], first, n_all))
        give(a["wxf"], per_view(a["wxf"], first, n_all))
    if plan.upright_back:
        give(a["obs_u"], per_view(a["obs_u"], first, plan.upright))
        give(a["wzb_u"], whole(a["wzb_u"]))
    if plan.turned_back:
        x = a["obs_t"]
        begin = first + n_up
        give(
            x,
            pl.BlockSpec(
                (x.shape[0], x.shape[1] // plan.turned) + x.shape[2:],
                lambda i: (0, jnp.clip(i - begin, 0, plan.turned - 1), 0, 0),
            ),
        )
        give(a["wzb_t"], whole(a["wzb_t"]))
        if not plan.forward:
            give(a["blurred"], per_view(a["blurred"], begin, plan.turned))
            for x in a["acc"]:
                give(x, pl.BlockSpec(memory_space=pl.ANY))
    backs = plan.upright if not plan.turned_back else n_all
    give(a["wxb"], per_view(a["wxb"], first, backs, shift))
    give(a["wyb"], per_view(a["wyb"], first, backs, shift))

    shapes = [
        jax.ShapeDtypeStruct((count * n, plan.width), F32)
        for n in (plan.rows, plan.side)
        for count in (plan.depth, plan.reach, plan.reach)
    ]
    out_specs = [whole(x) for x in shapes]
    if not plan.turned_back:
        x = jax.ShapeDtypeStruct((plan.turned, plan.depth * plan.rows, plan.width), F32)
        shapes.append(x)
        out_specs.append(per_view(x, first + n_up, plan.turned))
    scratch = []
    if plan.forward:
        scratch.append(pltpu.VMEM((n_all * plan.depth * (total + 2), plan.width), F32))
    scratch.append(pltpu.VMEM((total * (plan.lines + 8), plan.width), F32))
    if plan.turned_back and not plan.forward:
        scratch += [pltpu.VMEM(x.shape, F32) for x in a["acc"]]
        scratch.append(pltpu.SemaphoreType.DMA((len(a["acc"]),)))
    return pl.pallas_call(
        functools.partial(update_kernel, plan),
        out_shape=shapes,
        grid=(first + n_all + 1,),
        in_specs=specs,
        out_specs=out_specs,
        scratch_shapes=scratch,
        compiler_params=pltpu.CompilerParams(vmem_limit_bytes=plan.vmem),
        cost_estimate=pl.CostEstimate(
            flops=10**10, bytes_accessed=12 * 10**6, transcendentals=0
        ),
        name=plan.name,
    )(*args)


def pack_kernel(count, per, x, out):
    rows = x.shape[-1] // count
    for g in range(x.shape[0] // per):
        for d in range(count):
            out[d, g] = jnp.concatenate(
                [x[g * per + j, :, d * rows : (d + 1) * rows] for j in range(per)], axis=1
            )


def pack(turned, count, per):
    planes, xl, yf = turned.shape
    block = 48 if planes % 48 == 0 else per
    return pl.pallas_call(
        functools.partial(pack_kernel, count, per),
        out_shape=jax.ShapeDtypeStruct((count, planes // per, xl, per * (yf // count)), F32),
        grid=(planes // block,),
        in_specs=[pl.BlockSpec((block, xl, yf), lambda i: (i, 0, 0))],
        out_specs=pl.BlockSpec(
            (count, block // per, xl, per * (yf // count)), lambda i: (0, i, 0, 0)
        ),
        compiler_params=pltpu.CompilerParams(vmem_limit_bytes=VMEM_LIMIT),
        name="pack",
    )(turned)


def bands_kernel(plan, place, views_of, shift_x, kd, kr, kc, wzf, wyf, wxf, wxb, wyb, wzu, wzt):
    depth, rows, side, reach, zpad = plan.depth, plan.rows, plan.side, plan.reach, plan.zpad
    width = plan.width
    ypad = side // 2
    gap = zpad - reach
    active = views_of.shape[1]

    def taps(ref, v):
        row = ref[v : v + 1, :]
        row = row / jnp.sum(row, axis=1, keepdims=True)
        return jnp.concatenate([row, jnp.zeros((1, width - row.shape[1]), F32)], axis=1)

    def slide(row, height, amount):
        base = jnp.broadcast_to(row, (height, width))
        return pltpu.roll(base, amount, 1, stride=1, stride_axis=0)

    def parts(matrix):
        high = matrix.astype(BF16).astype(F32)
        return high, matrix - high

    def turn(matrix):
        rows_in, cols_in = matrix.shape
        square = jnp.concatenate([matrix, jnp.zeros((width - rows_in, cols_in), F32)], axis=0)
        square = jnp.concatenate([square, jnp.zeros((width, width - cols_in), F32)], axis=1)
        return square.T[:cols_in, :rows_in]

    def share(i, j, v):
        z = jnp.clip(place[0] + i - 1, 0, plan.n_gz - 1)
        y = jnp.clip(place[1] + j - 1, 0, plan.count - 1)
        found = jnp.int32(0)
        for k in range(active):
            found = found + (views_of[z * plan.count + y, k] == v).astype(jnp.int32)
        return found.astype(F32) / active

    place_z = lax.broadcasted_iota(jnp.int32, (depth + 2 * zpad, depth), 0)
    kept = []
    for v in range(plan.upright + plan.turned):
        wide = slide(taps(kd, v), depth, 0)
        zeros = jnp.zeros((depth, gap), F32)
        band = jnp.concatenate(
            [
                wide[:, :reach],
                zeros,
                wide[:, reach : reach + depth],
                wide[:, reach + depth : 2 * reach + depth],
                zeros,
            ],
            axis=1,
        )
        high, low = parts(band)
        wzf[v * depth : (v + 1) * depth, :] = jnp.concatenate([high, high, low], axis=1).astype(
            BF16
        )
        kept.append(turn(band))

        wide = slide(taps(kr, v), rows, ypad - plan.reach_y)
        band = jnp.concatenate(
            [wide[:, ypad : ypad + rows], wide[:, :ypad], wide[:, ypad + rows : 2 * ypad + rows]],
            axis=1,
        )
        high, low = parts(band)
        wyf[v] = jnp.concatenate(
            [
                jnp.concatenate([high, high], axis=1),
                jnp.concatenate([low, jnp.zeros_like(low)], axis=1),
            ],
            axis=0,
        ).astype(BF16)
        high, low = parts(turn(band))
        wyb[v] = jnp.concatenate([high, high, low], axis=1).astype(BF16)

        offset = plan.reach_x + shift_x[v]
        index = (
            lax.broadcasted_iota(jnp.int32, (width, width), 1)
            - lax.broadcasted_iota(jnp.int32, (width, width), 0)
            + offset
        )
        wide = pltpu.roll(slide(taps(kc, v), width, 0), width - offset, 1)
        band = jnp.where((index >= 0) & (index < kc.shape[1]), wide, 0.0)
        for out, matrix in ((wxb, band), (wxf, band.T)):
            high, low = parts(matrix)
            out[v, :width, :width] = high.astype(BF16)
            out[v, :width, width:] = low.astype(BF16)
            out[v, width:, :width] = high.astype(BF16)
            out[v, width:, width:] = jnp.zeros_like(low).astype(BF16)

    for out, begin, count in ((wzu, 0, plan.upright), (wzt, plan.upright, plan.turned)):
        for j in range(3):
            pieces = []
            for v in range(begin, begin + count):
                scale = jnp.where(
                    place_z < zpad,
                    share(0, j, v),
                    jnp.where(place_z < zpad + depth, share(1, j, v), share(2, j, v)),
                )
                pieces.append(kept[v] * scale)
            high, low = parts(jnp.concatenate(pieces, axis=1))
            out[j] = jnp.concatenate([high, high, low], axis=1).astype(BF16)


def bands(plan, place, views_of, shift_x, kd, kr, kc):
    views = plan.upright + plan.turned
    tall = plan.depth + 2 * plan.zpad
    total = plan.rows + plan.side
    shapes = [
        (views * plan.depth, 3 * tall),
        (views, 2 * plan.rows, 2 * total),
        (views, 2 * plan.width, 2 * plan.width),
        (views, 2 * plan.width, 2 * plan.width),
        (views, total, 3 * plan.rows),
        (3, tall, 3 * plan.upright * plan.depth),
        (3, tall, 3 * plan.turned * plan.depth),
    ]
    smem = pl.BlockSpec(memory_space=pltpu.SMEM)
    vmem = pl.BlockSpec(memory_space=pltpu.VMEM)
    return pl.pallas_call(
        functools.partial(bands_kernel, plan),
        out_shape=[jax.ShapeDtypeStruct(x, BF16) for x in shapes],
        in_specs=[smem] * 3 + [vmem] * 3,
        out_specs=[vmem] * len(shapes),
        compiler_params=pltpu.CompilerParams(vmem_limit_bytes=plan.vmem),
        name=plan.name,
    )(place, views_of, shift_x, kd, kr, kc)


def local(
    prior_estimate,
    views_upright,
    views_turned,
    kernel_depth,
    kernel_rows,
    kernel_columns,
    lateral_offsets,
    block_views,
):
    depth, rows, width = prior_estimate.shape
    views = kernel_depth.shape[0]
    reach = (kernel_depth.shape[1] - 1) // 2
    reach_y = (kernel_rows.shape[1] - 1) // 2
    reach_x = (kernel_columns.shape[1] - 1) // 2
    zpad = round_up(reach, 16)
    ypad = round_up(reach_y, 8)
    side = 2 * ypad
    n_xy = lax.axis_size("xy")
    n_gz = lax.axis_size("gz")

    half = views_turned.shape[0]
    per = width // rows
    packed = pack(
        views_turned.reshape(half * depth, views_turned.shape[2], views_turned.shape[3]), n_xy, per
    )
    upright = views_upright.reshape(views - half, depth * rows, width)

    n_up = views - half
    common = dict(
        depth=depth,
        rows=rows,
        side=side,
        reach=reach,
        zpad=zpad,
        width=width,
        upright=n_up,
        turned=half,
        per=per,
        count=n_xy,
        group=8,
        unroll=depth // 8,
    )
    plan = Plan(
        name="bands", vmem=56 << 20, n_gz=n_gz, reach_y=reach_y, reach_x=reach_x, **common
    )
    place = jnp.stack([lax.axis_index("gz"), lax.axis_index("xy")]).astype(jnp.int32)
    wz_f, wy_f, wx_f, wx_b, wy_b, wzb_u, wzb_t = bands(
        plan, place, block_views, lateral_offsets, kernel_depth, kernel_rows, kernel_columns
    )
    flat = lambda x: x.reshape(-1, width)
    cube = lambda x, n: x.reshape(-1, n, width)
    head = ((0, depth - reach), (0, 0), (0, 0))
    tail = ((depth - reach, 0), (0, 0), (0, 0))
    back = dict(wxb=wx_b, wyb=wy_b)
    ahead = dict(wzf=wz_f, wyf=wy_f, wxf=wx_f)
    estimate = prior_estimate
    for iteration in range(ITERS):
        from_left, from_right = exchange(
            estimate[:, :ypad], estimate[:, rows - ypad :], "xy"
        )
        source = estimate
        if iteration == 0:
            packed, source, from_left, from_right = lax.optimization_barrier(
                (packed, estimate, from_left, from_right)
            )
            received = lax.all_to_all(packed, "xy", split_axis=0, concat_axis=0, tiled=True)
        below, above = exchange(source[:reach], source[depth - reach :], "gz")
        sides = jnp.concatenate([from_left, from_right], axis=1)
        side_below, side_above = exchange(sides[:reach], sides[depth - reach :], "gz")
        volumes = [flat(x) for x in (estimate, below, above, sides, side_below, side_above)]
        if iteration == 0:
            *acc, blurred = update(
                Plan(
                    name="first", vmem=56 << 20, forward=True, upright_back=True, turned_back=False, **common
                ),
                volumes=volumes,
                obs_u=upright,
                wzb_u=wzb_u,
                **ahead,
                **back,
            )
            parts = update(
                Plan(
                    name="second", vmem=56 << 20, forward=False, upright_back=False, turned_back=True, **common
                ),
                obs_t=received,
                wzb_t=wzb_t,
                blurred=blurred,
                acc=acc,
                **back,
            )
        else:
            parts = update(
                Plan(name="both", vmem=36 << 20, forward=True, upright_back=True, turned_back=True, **common),
                volumes=volumes,
                obs_u=upright,
                obs_t=received,
                wzb_u=wzb_u,
                wzb_t=wzb_t,
                **ahead,
                **back,
            )
        cc, clo, chi = (cube(x, rows) for x in parts[:3])
        sc, slo, shi = (cube(x, side) for x in parts[3:])
        s_low, s_high = exchange(slo, shi, "gz")
        c_low, c_high = exchange(clo, chi, "gz")
        sc = sc + jnp.pad(s_low, head) + jnp.pad(s_high, tail)
        from_left, from_right = exchange(sc[:, :ypad], sc[:, ypad:], "xy")
        cc = cc + jnp.pad(c_low, head) + jnp.pad(c_high, tail)
        cc = cc + jnp.pad(from_left, ((0, 0), (0, rows - ypad), (0, 0)))
        cc = cc + jnp.pad(from_right, ((0, 0), (rows - ypad, 0), (0, 0)))
        estimate = estimate * cc
    return estimate


def solution(mesh):
    in_specs = (
        P("gz", "xy", None),
        P(None, "gz", "xy", None),
        P(None, "gz", "xy", None),
        P(),
        P(),
        P(),
        P(),
        P(),
    )
    out_specs = P("gz", "xy", None)
    return jax.shard_map(local, mesh=mesh, in_specs=in_specs, out_specs=out_specs, check_vma=False)
```

```python
import functools

import jax
import jax.numpy as jnp
from jax import lax
from jax.experimental import pallas as pl
from jax.experimental.pallas import tpu as pltpu
from jax.sharding import PartitionSpec as P

ITERS = 2
F32 = jnp.float32
BF16 = jnp.bfloat16
VMEM_LIMIT = 36 * 1024 * 1024
SPLIT = (56, 56, 36)


def round_up(value, unit):
    return -(-value // unit) * unit


def exchange(low, high, axis):
    count = lax.axis_size(axis)
    even = lax.axis_index(axis) % 2 == 0
    rounds = [
        [pair for i in range(begin, count - 1, 2) for pair in ((i, i + 1), (i + 1, i))]
        for begin in (0, 1)
    ]
    a = lax.ppermute(jnp.where(even, high, low), axis, rounds[0])
    b = lax.ppermute(jnp.where(even, low, high), axis, rounds[1])
    return jnp.where(even, b, a), jnp.where(even, a, b)


def halves(value):
    high = value.astype(BF16)
    low = (value - high.astype(F32)).astype(BF16)
    return high, low


def stack(value):
    top, rest = halves(value)
    return jnp.concatenate([top, rest, top], axis=0)


def update_kernel(plan, *refs):
    refs = list(refs)
    take = lambda n: [refs.pop(0) for _ in range(n)]
    depth, rows, side, reach, zpad = plan.depth, plan.rows, plan.side, plan.reach, plan.zpad
    width = plan.width
    total = rows + side
    pitch_c = rows + 2
    pitch_s = side + 2
    pitch_r = depth + 2
    if plan.forward:
        ahead_c, s, slo, shi, wzf, wyf, wxf = take(7)
    if plan.upright_back:
        obs_u, wzb_u = take(2)
    if plan.turned_back:
        obs_t, wzb_t = take(2)
        if not plan.forward:
            (blur_in,) = take(1)
            acc = take(3)
    wxb, wyb = take(2)
    outs = take(3)
    if plan.upright_back:
        (lines_u,) = take(1)
    if plan.turned_back:
        (lines_t,) = take(1)
    else:
        (blur_out,) = take(1)
    if plan.forward:
        (mid,) = take(1)
    (back,) = take(1)
    copies = []
    if plan.turned_back and not plan.forward:
        held = take(3)
        (arrived,) = take(1)
        copies = [
            pltpu.make_async_copy(x, y, arrived.at[i]) for i, (x, y) in enumerate(zip(acc, held))
        ]
        acc = held

        @pl.when(pl.program_id(0) == 0)
        def _():
            for copy in copies:
                copy.start()

    step = pl.program_id(0)
    first = 1 if plan.forward else 0
    n_up = plan.upright if (plan.forward) else 0
    n_all = n_up + plan.turned
    lines = plan.lines
    pitch_z = lines + 8
    group = plan.group

    if plan.forward:

        @pl.when(step == 0)
        def _():
            forward_z(plan, slo, s, shi, side, wzf, pitch_s, mid, n_all * depth)

    def blur_lines(view, i):
        pieces = []
        for j in range(group // 2):
            line = i * group + 2 * j
            both = jnp.concatenate(
                [
                    jnp.concatenate(
                        [
                            ahead_c[0, pl.ds((line + k) * pitch_c, rows), :],
                            mid[pl.ds((view * depth + line + k) * pitch_s, side), :],
                        ],
                        axis=0,
                    )
                    for k in range(2)
                ],
                axis=1,
            )
            top, rest = halves(both)
            result = jnp.dot(
                wyf[0], jnp.concatenate([top, rest], axis=0), preferred_element_type=F32
            )
            result = result[:rows] + result[rows:]
            pieces += [result[:, :width], result[:, width:]]
        top, rest = halves(jnp.concatenate(pieces, axis=0))
        result = jnp.dot(
            jnp.concatenate([top, rest], axis=1), wxf[0], preferred_element_type=F32
        )
        return result[:, :width] + result[:, width:]

    def spread_lines(slot, i, ratio, lines_c):
        top, rest = halves(ratio)
        flat = jnp.dot(jnp.concatenate([top, rest], axis=1), wxb[0], preferred_element_type=F32)
        flat = flat[:, :width] + flat[:, width:]
        for j in range(group // 2):
            both = jnp.concatenate(
                [flat[(2 * j + k) * rows : (2 * j + k + 1) * rows] for k in range(2)], axis=1
            )
            result = jnp.dot(wyb[0], stack(both), preferred_element_type=F32)
            for k in range(2):
                line = i * group + 2 * j + k
                piece = result[:, k * width : (k + 1) * width]
                lines_c[0, pl.ds(line, rows, stride=pitch_r), :] = piece[:rows]
                back[pl.ds(slot * depth + line, side, stride=pitch_z), :] = piece[rows:]

    def turned_lines(i):
        per = plan.per
        blocks = []
        for g in range(group // per):
            at = i * (group // per) + g
            blocks.append(jnp.concatenate([obs_t[k, at] for k in range(plan.count)], axis=0).T)
        return jnp.concatenate(blocks, axis=0)

    size = group * rows
    window = lambda i: pl.ds(pl.multiple_of(i * size, size), size)

    def loop(body):
        def wrapped(i, carry):
            body(i)
            return carry

        lax.fori_loop(0, depth // group, wrapped, 0, unroll=plan.unroll)

    if plan.upright_back:

        @pl.when((step >= first) & (step < first + n_up))
        def _():
            view = step - first

            def body(i):
                spread_lines(view, i, obs_u[0, window(i), :] / blur_lines(view, i), lines_u)

            loop(body)

    @pl.when((step >= first + n_up) & (step < first + n_all))
    def _():
        view = step - first

        def body(i):
            blurred = blur_lines(view, i) if plan.forward else blur_in[0, window(i), :]
            if plan.turned_back:
                spread_lines(view, i, turned_lines(i) / blurred, lines_t)
            else:
                blur_out[0, window(i), :] = blurred

        loop(body)

    @pl.when(step == first + n_all)
    def _():
        for copy in copies:
            copy.wait()
        banks = []
        if plan.upright_back:
            banks.append((wzb_u, 0, plan.upright * depth))
        if plan.turned_back:
            banks.append((wzb_t, n_up * depth, plan.turned * depth))

        def sums(y, region):
            result = None
            for weights, offset, count in banks:
                both = jnp.concatenate(
                    [back[pl.ds((y + j) * pitch_z + offset, count), :] for j in range(2)], axis=1
                )
                term = jnp.dot(weights[region], stack(both), preferred_element_type=F32)
                result = term if result is None else result + term
            return result

        adds = acc if (plan.turned_back and not plan.forward) else [None] * 3
        backward_z(plan, lambda y: sums(y, 0), outs, adds, side, 0, side // 4)
        backward_z(plan, lambda y: sums(y, 2), outs, adds, side, side // 4, side // 2)


def forward_z(plan, low, centre, high, n, weights, pitch, target, count):
    depth, reach = plan.depth, plan.reach
    width = plan.width
    fill = jnp.zeros((plan.zpad - reach, width), F32)

    def column(y):
        return jnp.concatenate(
            [
                low[pl.ds(y, reach, stride=n), :],
                fill,
                centre[pl.ds(y, depth, stride=n), :],
                high[pl.ds(y, reach, stride=n), :],
                fill,
            ],
            axis=0,
        )

    def body(i, carry):
        both = jnp.concatenate([column(2 * i + j) for j in range(2)], axis=1)
        result = jnp.dot(weights[...], stack(both), preferred_element_type=F32)
        for j in range(2):
            target[pl.ds(2 * i + j, count, stride=pitch), :] = result[
                :, j * width : (j + 1) * width
            ]
        return carry

    lax.fori_loop(0, n // 2, body, 0, unroll=8)


def backward_z(plan, sums, targets, adds, n, begin, end, shift=0):
    depth, reach, zpad, width = plan.depth, plan.reach, plan.zpad, plan.width

    def body(i, carry):
        result = sums(2 * i)
        for j in range(2):
            part = result[:, j * width : (j + 1) * width]
            for target, add, low, count in zip(
                targets, adds, (zpad, 0, zpad + depth), (depth, reach, reach)
            ):
                spot = (pl.ds(shift + 2 * i + j, count, stride=n), slice(None))
                piece = part[low : low + count]
                if add is not None:
                    piece = piece + add[spot]
                target[spot] = piece
        return carry

    lax.fori_loop(begin, end, body, 0, unroll=4)


def ahead_kernel(plan, c, clo, chi, wzf, out):
    forward_z(
        plan, clo, c, chi, plan.rows, wzf, plan.rows + 2, out, wzf.shape[0]
    )


def ahead(plan, c, clo, chi, wzf):
    cuts = 2
    whole = lambda x: pl.BlockSpec(x.shape, lambda i: (0, 0), pipeline_mode=pl.Buffered(1))
    lines = wzf.shape[0] * (plan.rows + 2)
    return pl.pallas_call(
        functools.partial(ahead_kernel, plan),
        out_shape=jax.ShapeDtypeStruct((lines, plan.width), F32),
        grid=(cuts,),
        in_specs=[whole(x) for x in (c, clo, chi)]
        + [pl.BlockSpec((wzf.shape[0] // cuts, wzf.shape[1]), lambda i: (i, 0))],
        out_specs=pl.BlockSpec((lines // cuts, plan.width), lambda i: (i, 0)),
        compiler_params=pltpu.CompilerParams(vmem_limit_bytes=plan.vmem),
        cost_estimate=pl.CostEstimate(flops=3 * 10**9, bytes_accessed=8 * 10**6, transcendentals=0),
        name=plan.name,
    )(c, clo, chi, wzf)


def behind_kernel(plan, span, ru, rt, wzu, wzt, cc, clo, chi):
    depth = plan.depth
    begin = pl.program_id(0) * span

    def sums(y):
        result = None
        for lines, weights in ((ru, wzu), (rt, wzt)):
            both = jnp.concatenate(
                [
                    jnp.concatenate(
                        [
                            lines[v, pl.ds((y + j) * (depth + 2), depth), :]
                            for v in range(lines.shape[0])
                        ],
                        axis=0,
                    )
                    for j in range(2)
                ],
                axis=1,
            )
            term = jnp.dot(weights[0], stack(both), preferred_element_type=F32)
            result = term if result is None else result + term
        return result

    backward_z(plan, sums, (cc, clo, chi), [None] * 3, plan.rows, 0, span // 2, begin)


def behind(plan, ru, rt, wzu, wzt):
    span = 8
    pitch = plan.depth + 2
    block = lambda x: pl.BlockSpec((x.shape[0], span * pitch, plan.width), lambda i: (0, i, 0))
    weights = lambda x: pl.BlockSpec((1,) + x.shape[1:], lambda i: (1, 0, 0))
    shapes = [
        jax.ShapeDtypeStruct((count * plan.rows, plan.width), F32)
        for count in (plan.depth, plan.reach, plan.reach)
    ]
    return pl.pallas_call(
        functools.partial(behind_kernel, plan, span),
        out_shape=shapes,
        grid=(plan.rows // span,),
        in_specs=[block(ru), block(rt), weights(wzu), weights(wzt)],
        out_specs=[
            pl.BlockSpec(x.shape, lambda i: (0, 0), pipeline_mode=pl.Buffered(1)) for x in shapes
        ],
        compiler_params=pltpu.CompilerParams(vmem_limit_bytes=plan.vmem),
        cost_estimate=pl.CostEstimate(flops=3 * 10**9, bytes_accessed=8 * 10**6, transcendentals=0),
        name=plan.name,
    )(ru, rt, wzu, wzt)


class Plan:
    def __init__(self, **fields):
        self.__dict__.update(fields)


def update(plan, **a):
    first = 1 if plan.forward else 0
    n_up = plan.upright if plan.forward else 0
    n_all = n_up + plan.turned
    used = (plan.upright if plan.upright_back else 0) + (plan.turned if plan.turned_back else 0)
    plan.lines = used * plan.depth
    shift = plan.upright - n_up
    once = pl.Buffered(1)

    def whole(x):
        return pl.BlockSpec(x.shape, lambda i: (0,) * len(x.shape), pipeline_mode=once)

    def per_view(x, start, count, offset=0):
        return pl.BlockSpec(
            (1,) + x.shape[1:],
            lambda i: (jnp.clip(i - start, 0, count - 1) + offset,) + (0,) * (len(x.shape) - 1),
        )

    args, specs = [], []

    def give(x, spec):
        args.append(x)
        specs.append(spec)

    if plan.forward:
        give(a["ahead_c"], per_view(a["ahead_c"], first, n_all))
        for x in a["volumes"]:
            give(x, whole(x))
        give(a["wzf"], whole(a["wzf"]))
        give(a["wyf"], per_view(a["wyf"], first, n_all))
        give(a["wxf"], per_view(a["wxf"], first, n_all))
    if plan.upright_back:
        give(a["obs_u"], per_view(a["obs_u"], first, plan.upright))
        give(a["wzb_u"], whole(a["wzb_u"]))
    if plan.turned_back:
        x = a["obs_t"]
        begin = first + n_up
        give(
            x,
            pl.BlockSpec(
                (x.shape[0], x.shape[1] // plan.turned) + x.shape[2:],
                lambda i: (0, jnp.clip(i - begin, 0, plan.turned - 1), 0, 0),
            ),
        )
        give(a["wzb_t"], whole(a["wzb_t"]))
        if not plan.forward:
            give(a["blurred"], per_view(a["blurred"], begin, plan.turned))
            for x in a["acc"]:
                give(x, pl.BlockSpec(memory_space=pl.ANY))
    backs = plan.upright if not plan.turned_back else n_all
    give(a["wxb"], per_view(a["wxb"], first, backs, shift))
    give(a["wyb"], per_view(a["wyb"], first, backs, shift))

    shapes = [
        jax.ShapeDtypeStruct((count * n, plan.width), F32)
        for n in (plan.side,)
        for count in (plan.depth, plan.reach, plan.reach)
    ]
    out_specs = [whole(x) for x in shapes]
    for used, begin, count in (
        (plan.upright_back, first, plan.upright),
        (plan.turned_back, first + n_up, plan.turned),
    ):
        if used:
            x = jax.ShapeDtypeStruct((count, plan.rows * (plan.depth + 2), plan.width), F32)
            shapes.append(x)
            out_specs.append(per_view(x, begin, count))
    if not plan.turned_back:
        x = jax.ShapeDtypeStruct((plan.turned, plan.depth * plan.rows, plan.width), F32)
        shapes.append(x)
        out_specs.append(per_view(x, first + n_up, plan.turned))
    scratch = []
    if plan.forward:
        scratch.append(pltpu.VMEM((n_all * plan.depth * (plan.side + 2), plan.width), F32))
    scratch.append(pltpu.VMEM((plan.side * (plan.lines + 8), plan.width), F32))
    if plan.turned_back and not plan.forward:
        scratch += [pltpu.VMEM(x.shape, F32) for x in a["acc"]]
        scratch.append(pltpu.SemaphoreType.DMA((len(a["acc"]),)))
    return pl.pallas_call(
        functools.partial(update_kernel, plan),
        out_shape=shapes,
        grid=(first + n_all + 1,),
        in_specs=specs,
        out_specs=out_specs,
        scratch_shapes=scratch,
        compiler_params=pltpu.CompilerParams(vmem_limit_bytes=plan.vmem),
        cost_estimate=pl.CostEstimate(
            flops=10**10, bytes_accessed=12 * 10**6, transcendentals=0
        ),
        name=plan.name,
    )(*args)


def pack_kernel(count, per, x, out):
    rows = x.shape[-1] // count
    for g in range(x.shape[0] // per):
        for d in range(count):
            out[d, g] = jnp.concatenate(
                [x[g * per + j, :, d * rows : (d + 1) * rows] for j in range(per)], axis=1
            )


def pack(turned, count, per):
    planes, xl, yf = turned.shape
    block = 48 if planes % 48 == 0 else per
    return pl.pallas_call(
        functools.partial(pack_kernel, count, per),
        out_shape=jax.ShapeDtypeStruct((count, planes // per, xl, per * (yf // count)), F32),
        grid=(planes // block,),
        in_specs=[pl.BlockSpec((block, xl, yf), lambda i: (i, 0, 0))],
        out_specs=pl.BlockSpec(
            (count, block // per, xl, per * (yf // count)), lambda i: (0, i, 0, 0)
        ),
        compiler_params=pltpu.CompilerParams(vmem_limit_bytes=VMEM_LIMIT),
        name="pack",
    )(turned)


def bands_kernel(plan, place, views_of, shift_x, kd, kr, kc, wzf, wyf, wxf, wxb, wyb, wzu, wzt):
    depth, rows, side, reach, zpad = plan.depth, plan.rows, plan.side, plan.reach, plan.zpad
    width = plan.width
    ypad = side // 2
    gap = zpad - reach
    active = views_of.shape[1]

    def taps(ref, v):
        row = ref[v : v + 1, :]
        row = row / jnp.sum(row, axis=1, keepdims=True)
        return jnp.concatenate([row, jnp.zeros((1, width - row.shape[1]), F32)], axis=1)

    def slide(row, height, amount):
        base = jnp.broadcast_to(row, (height, width))
        return pltpu.roll(base, amount, 1, stride=1, stride_axis=0)

    def parts(matrix):
        high = matrix.astype(BF16).astype(F32)
        return high, matrix - high

    def turn(matrix):
        rows_in, cols_in = matrix.shape
        square = jnp.concatenate([matrix, jnp.zeros((width - rows_in, cols_in), F32)], axis=0)
        square = jnp.concatenate([square, jnp.zeros((width, width - cols_in), F32)], axis=1)
        return square.T[:cols_in, :rows_in]

    def share(i, j, v):
        z = jnp.clip(place[0] + i - 1, 0, plan.n_gz - 1)
        y = jnp.clip(place[1] + j - 1, 0, plan.count - 1)
        found = jnp.int32(0)
        for k in range(active):
            found = found + (views_of[z * plan.count + y, k] == v).astype(jnp.int32)
        return found.astype(F32) / active

    place_z = lax.broadcasted_iota(jnp.int32, (depth + 2 * zpad, depth), 0)
    kept = []
    for v in range(plan.upright + plan.turned):
        wide = slide(taps(kd, v), depth, 0)
        zeros = jnp.zeros((depth, gap), F32)
        band = jnp.concatenate(
            [
                wide[:, :reach],
                zeros,
                wide[:, reach : reach + depth],
                wide[:, reach + depth : 2 * reach + depth],
                zeros,
            ],
            axis=1,
        )
        high, low = parts(band)
        wzf[v * depth : (v + 1) * depth, :] = jnp.concatenate([high, high, low], axis=1).astype(
            BF16
        )
        kept.append(turn(band))

        wide = slide(taps(kr, v), rows, ypad - plan.reach_y)
        band = jnp.concatenate(
            [wide[:, ypad : ypad + rows], wide[:, :ypad], wide[:, ypad + rows : 2 * ypad + rows]],
            axis=1,
        )
        high, low = parts(band)
        wyf[v] = jnp.concatenate(
            [
                jnp.concatenate([high, high], axis=1),
                jnp.concatenate([low, jnp.zeros_like(low)], axis=1),
            ],
            axis=0,
        ).astype(BF16)
        high, low = parts(turn(band))
        wyb[v] = jnp.concatenate([high, high, low], axis=1).astype(BF16)

        offset = plan.reach_x + shift_x[v]
        index = (
            lax.broadcasted_iota(jnp.int32, (width, width), 1)
            - lax.broadcasted_iota(jnp.int32, (width, width), 0)
            + offset
        )
        wide = pltpu.roll(slide(taps(kc, v), width, 0), width - offset, 1)
        band = jnp.where((index >= 0) & (index < kc.shape[1]), wide, 0.0)
        for out, matrix in ((wxb, band), (wxf, band.T)):
            high, low = parts(matrix)
            out[v, :width, :width] = high.astype(BF16)
            out[v, :width, width:] = low.astype(BF16)
            out[v, width:, :width] = high.astype(BF16)
            out[v, width:, width:] = jnp.zeros_like(low).astype(BF16)

    for out, begin, count in ((wzu, 0, plan.upright), (wzt, plan.upright, plan.turned)):
        for j in range(3):
            pieces = []
            for v in range(begin, begin + count):
                scale = jnp.where(
                    place_z < zpad,
                    share(0, j, v),
                    jnp.where(place_z < zpad + depth, share(1, j, v), share(2, j, v)),
                )
                pieces.append(kept[v] * scale)
            high, low = parts(jnp.concatenate(pieces, axis=1))
            out[j] = jnp.concatenate([high, high, low], axis=1).astype(BF16)


def bands(plan, place, views_of, shift_x, kd, kr, kc):
    views = plan.upright + plan.turned
    tall = plan.depth + 2 * plan.zpad
    total = plan.rows + plan.side
    shapes = [
        (views * plan.depth, 3 * tall),
        (views, 2 * plan.rows, 2 * total),
        (views, 2 * plan.width, 2 * plan.width),
        (views, 2 * plan.width, 2 * plan.width),
        (views, total, 3 * plan.rows),
        (3, tall, 3 * plan.upright * plan.depth),
        (3, tall, 3 * plan.turned * plan.depth),
    ]
    smem = pl.BlockSpec(memory_space=pltpu.SMEM)
    vmem = pl.BlockSpec(memory_space=pltpu.VMEM)
    return pl.pallas_call(
        functools.partial(bands_kernel, plan),
        out_shape=[jax.ShapeDtypeStruct(x, BF16) for x in shapes],
        in_specs=[smem] * 3 + [vmem] * 3,
        out_specs=[vmem] * len(shapes),
        compiler_params=pltpu.CompilerParams(vmem_limit_bytes=plan.vmem),
        name=plan.name,
    )(place, views_of, shift_x, kd, kr, kc)


def local(
    prior_estimate,
    views_upright,
    views_turned,
    kernel_depth,
    kernel_rows,
    kernel_columns,
    lateral_offsets,
    block_views,
):
    depth, rows, width = prior_estimate.shape
    views = kernel_depth.shape[0]
    reach = (kernel_depth.shape[1] - 1) // 2
    reach_y = (kernel_rows.shape[1] - 1) // 2
    reach_x = (kernel_columns.shape[1] - 1) // 2
    zpad = round_up(reach, 16)
    ypad = round_up(reach_y, 8)
    side = 2 * ypad
    n_xy = lax.axis_size("xy")
    n_gz = lax.axis_size("gz")

    half = views_turned.shape[0]
    per = width // rows
    packed = pack(
        views_turned.reshape(half * depth, views_turned.shape[2], views_turned.shape[3]), n_xy, per
    )
    upright = views_upright.reshape(views - half, depth * rows, width)

    n_up = views - half
    common = dict(
        depth=depth,
        rows=rows,
        side=side,
        reach=reach,
        zpad=zpad,
        width=width,
        upright=n_up,
        turned=half,
        per=per,
        count=n_xy,
        group=8,
        unroll=depth // 8,
    )
    plan = Plan(
        name="bands", vmem=56 << 20, n_gz=n_gz, reach_y=reach_y, reach_x=reach_x, **common
    )
    place = jnp.stack([lax.axis_index("gz"), lax.axis_index("xy")]).astype(jnp.int32)
    wz_f, wy_f, wx_f, wx_b, wy_b, wzb_u, wzb_t = bands(
        plan, place, block_views, lateral_offsets, kernel_depth, kernel_rows, kernel_columns
    )
    flat = lambda x: x.reshape(-1, width)
    cube = lambda x, n: x.reshape(-1, n, width)
    head = ((0, depth - reach), (0, 0), (0, 0))
    tail = ((depth - reach, 0), (0, 0), (0, 0))
    back = dict(wxb=wx_b, wyb=wy_b)
    shared = dict(wzf=wz_f, wyf=wy_f, wxf=wx_f)
    estimate = prior_estimate
    for iteration in range(ITERS):
        from_left, from_right = exchange(
            estimate[:, :ypad], estimate[:, rows - ypad :], "xy"
        )
        if iteration == 0:
            packed, from_left, from_right = lax.optimization_barrier(
                (packed, from_left, from_right)
            )
            received = lax.all_to_all(packed, "xy", split_axis=0, concat_axis=0, tiled=True)
        below, above = exchange(estimate[:reach], estimate[depth - reach :], "gz")
        sides = jnp.concatenate([from_left, from_right], axis=1)
        side_below, side_above = exchange(sides[:reach], sides[depth - reach :], "gz")
        early = ahead(
            Plan(name="ahead", vmem=24 << 20, **common),
            flat(estimate),
            flat(below),
            flat(above),
            wz_f,
        )
        volumes = [flat(x) for x in (sides, side_below, side_above)]
        forth = dict(ahead_c=early.reshape(views, -1, width), volumes=volumes, **shared)
        if iteration == 0:
            *acc, lines_u, blurred = update(
                Plan(
                    name="first",
                    vmem=SPLIT[0] << 20,
                    forward=True,
                    upright_back=True,
                    turned_back=False,
                    **common,
                ),
                obs_u=upright,
                wzb_u=wzb_u,
                **forth,
                **back,
            )
            *parts, lines_t = update(
                Plan(
                    name="second",
                    vmem=SPLIT[1] << 20,
                    forward=False,
                    upright_back=False,
                    turned_back=True,
                    **common,
                ),
                obs_t=received,
                wzb_t=wzb_t,
                blurred=blurred,
                acc=acc,
                **back,
            )
        else:
            *parts, lines_u, lines_t = update(
                Plan(
                    name="both",
                    vmem=SPLIT[2] << 20,
                    forward=True,
                    upright_back=True,
                    turned_back=True,
                    **common,
                ),
                obs_u=upright,
                obs_t=received,
                wzb_u=wzb_u,
                wzb_t=wzb_t,
                **forth,
                **back,
            )
        sc, slo, shi = (cube(x, side) for x in parts)
        cc, clo, chi = (
            cube(x, rows)
            for x in behind(
                Plan(name="behind", vmem=24 << 20, **common), lines_u, lines_t, wzb_u, wzb_t
            )
        )
        s_low, s_high = exchange(slo, shi, "gz")
        c_low, c_high = exchange(clo, chi, "gz")
        sc = sc + jnp.pad(s_low, head) + jnp.pad(s_high, tail)
        from_left, from_right = exchange(sc[:, :ypad], sc[:, ypad:], "xy")
        cc = cc + jnp.pad(c_low, head) + jnp.pad(c_high, tail)
        cc = cc + jnp.pad(from_left, ((0, 0), (0, rows - ypad), (0, 0)))
        cc = cc + jnp.pad(from_right, ((0, 0), (rows - ypad, 0), (0, 0)))
        estimate = estimate * cc
    return estimate


def solution(mesh):
    in_specs = (
        P("gz", "xy", None),
        P(None, "gz", "xy", None),
        P(None, "gz", "xy", None),
        P(),
        P(),
        P(),
        P(),
        P(),
    )
    out_specs = P("gz", "xy", None)
    return jax.shard_map(local, mesh=mesh, in_specs=in_specs, out_specs=out_specs, check_vma=False)
```

```python
import functools

import jax
import jax.numpy as jnp
from jax import lax
from jax.experimental import pallas as pl
from jax.experimental.pallas import tpu as pltpu
from jax.sharding import PartitionSpec as P

ITERS = 2
F32 = jnp.float32
BF16 = jnp.bfloat16
VMEM_LIMIT = 36 * 1024 * 1024
SPLIT = (56, 56, 36)


def round_up(value, unit):
    return -(-value // unit) * unit


def exchange(low, high, axis):
    count = lax.axis_size(axis)
    even = lax.axis_index(axis) % 2 == 0
    rounds = [
        [pair for i in range(begin, count - 1, 2) for pair in ((i, i + 1), (i + 1, i))]
        for begin in (0, 1)
    ]
    a = lax.ppermute(jnp.where(even, high, low), axis, rounds[0])
    b = lax.ppermute(jnp.where(even, low, high), axis, rounds[1])
    return jnp.where(even, b, a), jnp.where(even, a, b)


def halves(value):
    high = value.astype(BF16)
    low = (value - high.astype(F32)).astype(BF16)
    return high, low


def stack(value):
    top, rest = halves(value)
    return jnp.concatenate([top, rest, top], axis=0)


def update_kernel(plan, *refs):
    refs = list(refs)
    take = lambda n: [refs.pop(0) for _ in range(n)]
    depth, rows, side, reach, zpad = plan.depth, plan.rows, plan.side, plan.reach, plan.zpad
    width = plan.width
    total = rows + side
    pitch_c = rows + 2
    pitch_s = side + 2
    pitch_r = depth + 2
    if plan.forward:
        ahead_c, s, slo, shi, wzf, wyf, wxf = take(7)
    if plan.upright_back:
        obs_u, wzb_u = take(2)
    if plan.turned_back:
        obs_t, wzb_t = take(2)
        if not plan.forward:
            (blur_in,) = take(1)
            acc = take(3)
    wxb, wyb = take(2)
    outs = take(3)
    if plan.upright_back:
        (lines_u,) = take(1)
    if plan.turned_back:
        (lines_t,) = take(1)
    else:
        (blur_out,) = take(1)
    if plan.forward:
        (mid,) = take(1)
    (back,) = take(1)
    copies = []
    if plan.turned_back and not plan.forward:
        held = take(3)
        (arrived,) = take(1)
        copies = [
            pltpu.make_async_copy(x, y, arrived.at[i]) for i, (x, y) in enumerate(zip(acc, held))
        ]
        acc = held

        @pl.when(pl.program_id(0) == 0)
        def _():
            for copy in copies:
                copy.start()

    step = pl.program_id(0)
    first = 1 if plan.forward else 0
    n_up = plan.upright if (plan.forward) else 0
    n_all = n_up + plan.turned
    lines = plan.lines
    pitch_z = lines + 8
    group = plan.group

    if plan.forward:

        @pl.when(step == 0)
        def _():
            forward_z(plan, slo, s, shi, side, wzf, pitch_s, mid, n_all * depth)

    def blur_lines(view, i):
        pieces = []
        for j in range(group // 2):
            line = i * group + 2 * j
            both = jnp.concatenate(
                [
                    jnp.concatenate(
                        [
                            ahead_c[0, pl.ds((line + k) * pitch_c, rows), :],
                            mid[pl.ds((view * depth + line + k) * pitch_s, side), :],
                        ],
                        axis=0,
                    )
                    for k in range(2)
                ],
                axis=1,
            )
            top, rest = halves(both)
            result = jnp.dot(
                wyf[0], jnp.concatenate([top, rest], axis=0), preferred_element_type=F32
            )
            result = result[:rows] + result[rows:]
            pieces += [result[:, :width], result[:, width:]]
        top, rest = halves(jnp.concatenate(pieces, axis=0))
        result = jnp.dot(
            jnp.concatenate([top, rest], axis=1), wxf[0], preferred_element_type=F32
        )
        return result[:, :width] + result[:, width:]

    def spread_lines(slot, i, ratio, lines_c):
        top, rest = halves(ratio)
        flat = jnp.dot(jnp.concatenate([top, rest], axis=1), wxb[0], preferred_element_type=F32)
        flat = flat[:, :width] + flat[:, width:]
        for j in range(group // 2):
            both = jnp.concatenate(
                [flat[(2 * j + k) * rows : (2 * j + k + 1) * rows] for k in range(2)], axis=1
            )
            result = jnp.dot(wyb[0], stack(both), preferred_element_type=F32)
            for k in range(2):
                line = i * group + 2 * j + k
                piece = result[:, k * width : (k + 1) * width]
                lines_c[0, pl.ds(line, rows, stride=pitch_r), :] = piece[:rows]
                back[pl.ds(slot * depth + line, side, stride=pitch_z), :] = piece[rows:]

    def turned_lines(i):
        per = plan.per
        blocks = []
        for g in range(group // per):
            at = i * (group // per) + g
            blocks.append(jnp.concatenate([obs_t[k, at] for k in range(plan.count)], axis=0).T)
        return jnp.concatenate(blocks, axis=0)

    size = group * rows
    window = lambda i: pl.ds(pl.multiple_of(i * size, size), size)

    def loop(body):
        def wrapped(i, carry):
            body(i)
            return carry

        lax.fori_loop(0, depth // group, wrapped, 0, unroll=plan.unroll)

    if plan.upright_back:

        @pl.when((step >= first) & (step < first + n_up))
        def _():
            view = step - first

            def body(i):
                spread_lines(view, i, obs_u[0, window(i), :] / blur_lines(view, i), lines_u)

            loop(body)

    @pl.when((step >= first + n_up) & (step < first + n_all))
    def _():
        view = step - first

        def body(i):
            blurred = blur_lines(view, i) if plan.forward else blur_in[0, window(i), :]
            if plan.turned_back:
                spread_lines(view, i, turned_lines(i) / blurred, lines_t)
            else:
                blur_out[0, window(i), :] = blurred

        loop(body)

    @pl.when(step == first + n_all)
    def _():
        for copy in copies:
            copy.wait()
        banks = []
        if plan.upright_back:
            banks.append((wzb_u, 0, plan.upright * depth))
        if plan.turned_back:
            banks.append((wzb_t, n_up * depth, plan.turned * depth))

        def sums(y, region):
            result = None
            for weights, offset, count in banks:
                both = jnp.concatenate(
                    [back[pl.ds((y + j) * pitch_z + offset, count), :] for j in range(2)], axis=1
                )
                term = jnp.dot(weights[region], stack(both), preferred_element_type=F32)
                result = term if result is None else result + term
            return result

        adds = acc if (plan.turned_back and not plan.forward) else [None] * 3
        backward_z(plan, lambda y: sums(y, 0), outs, adds, side, 0, side // 4)
        backward_z(plan, lambda y: sums(y, 2), outs, adds, side, side // 4, side // 2)


def forward_z(plan, low, centre, high, n, weights, pitch, target, count):
    depth, reach = plan.depth, plan.reach
    width = plan.width
    fill = jnp.zeros((plan.zpad - reach, width), F32)

    def column(y):
        return jnp.concatenate(
            [
                low[pl.ds(y, reach, stride=n), :],
                fill,
                centre[pl.ds(y, depth, stride=n), :],
                high[pl.ds(y, reach, stride=n), :],
                fill,
            ],
            axis=0,
        )

    def body(i, carry):
        both = jnp.concatenate([column(2 * i + j) for j in range(2)], axis=1)
        result = jnp.dot(weights[...], stack(both), preferred_element_type=F32)
        for j in range(2):
            target[pl.ds(2 * i + j, count, stride=pitch), :] = result[
                :, j * width : (j + 1) * width
            ]
        return carry

    lax.fori_loop(0, n // 2, body, 0, unroll=8)


def backward_z(plan, sums, targets, adds, n, begin, end, shift=0):
    depth, reach, zpad, width = plan.depth, plan.reach, plan.zpad, plan.width

    def body(i, carry):
        result = sums(2 * i)
        for j in range(2):
            part = result[:, j * width : (j + 1) * width]
            for target, add, low, count in zip(
                targets, adds, (zpad, 0, zpad + depth), (depth, reach, reach)
            ):
                spot = (pl.ds(shift + 2 * i + j, count, stride=n), slice(None))
                piece = part[low : low + count]
                if add is not None:
                    piece = piece + add[spot]
                target[spot] = piece
        return carry

    lax.fori_loop(begin, end, body, 0, unroll=4)


def ahead_kernel(plan, c, clo, chi, wzf, out):
    forward_z(
        plan, clo, c, chi, plan.rows, wzf, plan.rows + 2, out, wzf.shape[0]
    )


def ahead(plan, c, clo, chi, wzf):
    cuts = 2
    whole = lambda x: pl.BlockSpec(x.shape, lambda i: (0, 0), pipeline_mode=pl.Buffered(1))
    lines = wzf.shape[0] * (plan.rows + 2)
    return pl.pallas_call(
        functools.partial(ahead_kernel, plan),
        out_shape=jax.ShapeDtypeStruct((lines, plan.width), F32),
        grid=(cuts,),
        in_specs=[whole(x) for x in (c, clo, chi)]
        + [pl.BlockSpec((wzf.shape[0] // cuts, wzf.shape[1]), lambda i: (i, 0))],
        out_specs=pl.BlockSpec((lines // cuts, plan.width), lambda i: (i, 0)),
        compiler_params=pltpu.CompilerParams(vmem_limit_bytes=plan.vmem),
        cost_estimate=pl.CostEstimate(flops=3 * 10**9, bytes_accessed=8 * 10**6, transcendentals=0),
        name=plan.name,
    )(c, clo, chi, wzf)


def behind_kernel(plan, span, ru, rt, wzu, wzt, cc, clo, chi):
    depth = plan.depth
    begin = pl.program_id(0) * span

    def sums(y):
        result = None
        for lines, weights in ((ru, wzu), (rt, wzt)):
            both = jnp.concatenate(
                [
                    jnp.concatenate(
                        [
                            lines[v, pl.ds((y + j) * (depth + 2), depth), :]
                            for v in range(lines.shape[0])
                        ],
                        axis=0,
                    )
                    for j in range(2)
                ],
                axis=1,
            )
            term = jnp.dot(weights[0], stack(both), preferred_element_type=F32)
            result = term if result is None else result + term
        return result

    backward_z(plan, sums, (cc, clo, chi), [None] * 3, plan.rows, 0, span // 2, begin)


def behind(plan, ru, rt, wzu, wzt):
    span = 8
    pitch = plan.depth + 2
    block = lambda x: pl.BlockSpec((x.shape[0], span * pitch, plan.width), lambda i: (0, i, 0))
    weights = lambda x: pl.BlockSpec((1,) + x.shape[1:], lambda i: (1, 0, 0))
    shapes = [
        jax.ShapeDtypeStruct((count * plan.rows, plan.width), F32)
        for count in (plan.depth, plan.reach, plan.reach)
    ]
    return pl.pallas_call(
        functools.partial(behind_kernel, plan, span),
        out_shape=shapes,
        grid=(plan.rows // span,),
        in_specs=[block(ru), block(rt), weights(wzu), weights(wzt)],
        out_specs=[
            pl.BlockSpec(x.shape, lambda i: (0, 0), pipeline_mode=pl.Buffered(1)) for x in shapes
        ],
        compiler_params=pltpu.CompilerParams(vmem_limit_bytes=plan.vmem),
        cost_estimate=pl.CostEstimate(flops=3 * 10**9, bytes_accessed=8 * 10**6, transcendentals=0),
        name=plan.name,
    )(ru, rt, wzu, wzt)


class Plan:
    def __init__(self, **fields):
        self.__dict__.update(fields)


def update(plan, **a):
    first = 1 if plan.forward else 0
    n_up = plan.upright if plan.forward else 0
    n_all = n_up + plan.turned
    used = (plan.upright if plan.upright_back else 0) + (plan.turned if plan.turned_back else 0)
    plan.lines = used * plan.depth
    shift = plan.upright - n_up
    once = pl.Buffered(1)

    def whole(x):
        return pl.BlockSpec(x.shape, lambda i: (0,) * len(x.shape), pipeline_mode=once)

    def per_view(x, start, count, offset=0):
        return pl.BlockSpec(
            (1,) + x.shape[1:],
            lambda i: (jnp.clip(i - start, 0, count - 1) + offset,) + (0,) * (len(x.shape) - 1),
        )

    args, specs = [], []

    def give(x, spec):
        args.append(x)
        specs.append(spec)

    if plan.forward:
        give(a["ahead_c"], per_view(a["ahead_c"], first, n_all))
        for x in a["volumes"]:
            give(x, whole(x))
        give(a["wzf"], whole(a["wzf"]))
        give(a["wyf"], per_view(a["wyf"], first, n_all))
        give(a["wxf"], per_view(a["wxf"], first, n_all))
    if plan.upright_back:
        give(a["obs_u"], per_view(a["obs_u"], first, plan.upright))
        give(a["wzb_u"], whole(a["wzb_u"]))
    if plan.turned_back:
        x = a["obs_t"]
        begin = first + n_up
        give(
            x,
            pl.BlockSpec(
                (x.shape[0], x.shape[1] // plan.turned) + x.shape[2:],
                lambda i: (0, jnp.clip(i - begin, 0, plan.turned - 1), 0, 0),
            ),
        )
        give(a["wzb_t"], whole(a["wzb_t"]))
        if not plan.forward:
            give(a["blurred"], per_view(a["blurred"], begin, plan.turned))
            for x in a["acc"]:
                give(x, pl.BlockSpec(memory_space=pl.ANY))
    backs = plan.upright if not plan.turned_back else n_all
    give(a["wxb"], per_view(a["wxb"], first, backs, shift))
    give(a["wyb"], per_view(a["wyb"], first, backs, shift))

    shapes = [
        jax.ShapeDtypeStruct((count * n, plan.width), F32)
        for n in (plan.side,)
        for count in (plan.depth, plan.reach, plan.reach)
    ]
    out_specs = [whole(x) for x in shapes]
    for used, begin, count in (
        (plan.upright_back, first, plan.upright),
        (plan.turned_back, first + n_up, plan.turned),
    ):
        if used:
            x = jax.ShapeDtypeStruct((count, plan.rows * (plan.depth + 2), plan.width), F32)
            shapes.append(x)
            out_specs.append(per_view(x, begin, count))
    if not plan.turned_back:
        x = jax.ShapeDtypeStruct((plan.turned, plan.depth * plan.rows, plan.width), F32)
        shapes.append(x)
        out_specs.append(per_view(x, first + n_up, plan.turned))
    scratch = []
    if plan.forward:
        scratch.append(pltpu.VMEM((n_all * plan.depth * (plan.side + 2), plan.width), F32))
    scratch.append(pltpu.VMEM((plan.side * (plan.lines + 8), plan.width), F32))
    if plan.turned_back and not plan.forward:
        scratch += [pltpu.VMEM(x.shape, F32) for x in a["acc"]]
        scratch.append(pltpu.SemaphoreType.DMA((len(a["acc"]),)))
    return pl.pallas_call(
        functools.partial(update_kernel, plan),
        out_shape=shapes,
        grid=(first + n_all + 1,),
        in_specs=specs,
        out_specs=out_specs,
        scratch_shapes=scratch,
        compiler_params=pltpu.CompilerParams(vmem_limit_bytes=plan.vmem),
        cost_estimate=pl.CostEstimate(
            flops=10**10, bytes_accessed=12 * 10**6, transcendentals=0
        ),
        name=plan.name,
    )(*args)


def pack_kernel(count, per, x, out):
    rows = x.shape[-1] // count
    for g in range(x.shape[0] // per):
        for d in range(count):
            out[d, g] = jnp.concatenate(
                [x[g * per + j, :, d * rows : (d + 1) * rows] for j in range(per)], axis=1
            )


def pack(turned, count, per):
    planes, xl, yf = turned.shape
    block = 48 if planes % 48 == 0 else per
    return pl.pallas_call(
        functools.partial(pack_kernel, count, per),
        out_shape=jax.ShapeDtypeStruct((count, planes // per, xl, per * (yf // count)), F32),
        grid=(planes // block,),
        in_specs=[pl.BlockSpec((block, xl, yf), lambda i: (i, 0, 0))],
        out_specs=pl.BlockSpec(
            (count, block // per, xl, per * (yf // count)), lambda i: (0, i, 0, 0)
        ),
        compiler_params=pltpu.CompilerParams(vmem_limit_bytes=VMEM_LIMIT),
        name="pack",
    )(turned)


def bands_kernel(plan, place, views_of, shift_x, kd, kr, kc, wzf, wyf, wxf, wxb, wyb, wzu, wzt):
    depth, rows, side, reach, zpad = plan.depth, plan.rows, plan.side, plan.reach, plan.zpad
    width = plan.width
    ypad = side // 2
    gap = zpad - reach
    active = views_of.shape[1]

    def taps(ref, v):
        row = ref[v : v + 1, :]
        row = row / jnp.sum(row, axis=1, keepdims=True)
        return jnp.concatenate([row, jnp.zeros((1, width - row.shape[1]), F32)], axis=1)

    def slide(row, height, amount):
        base = jnp.broadcast_to(row, (height, width))
        return pltpu.roll(base, amount, 1, stride=1, stride_axis=0)

    def parts(matrix):
        high = matrix.astype(BF16).astype(F32)
        return high, matrix - high

    def turn(matrix):
        rows_in, cols_in = matrix.shape
        square = jnp.concatenate([matrix, jnp.zeros((width - rows_in, cols_in), F32)], axis=0)
        square = jnp.concatenate([square, jnp.zeros((width, width - cols_in), F32)], axis=1)
        return square.T[:cols_in, :rows_in]

    def share(i, j, v):
        z = jnp.clip(place[0] + i - 1, 0, plan.n_gz - 1)
        y = jnp.clip(place[1] + j - 1, 0, plan.count - 1)
        found = jnp.int32(0)
        for k in range(active):
            found = found + (views_of[z * plan.count + y, k] == v).astype(jnp.int32)
        return found.astype(F32) / active

    place_z = lax.broadcasted_iota(jnp.int32, (depth + 2 * zpad, depth), 0)
    kept = []
    for v in range(plan.upright + plan.turned):
        wide = slide(taps(kd, v), depth, 0)
        zeros = jnp.zeros((depth, gap), F32)
        band = jnp.concatenate(
            [
                wide[:, :reach],
                zeros,
                wide[:, reach : reach + depth],
                wide[:, reach + depth : 2 * reach + depth],
                zeros,
            ],
            axis=1,
        )
        high, low = parts(band)
        wzf[v * depth : (v + 1) * depth, :] = jnp.concatenate([high, high, low], axis=1).astype(
            BF16
        )
        kept.append(turn(band))

        wide = slide(taps(kr, v), rows, ypad - plan.reach_y)
        band = jnp.concatenate(
            [wide[:, ypad : ypad + rows], wide[:, :ypad], wide[:, ypad + rows : 2 * ypad + rows]],
            axis=1,
        )
        high, low = parts(band)
        wyf[v] = jnp.concatenate(
            [
                jnp.concatenate([high, high], axis=1),
                jnp.concatenate([low, jnp.zeros_like(low)], axis=1),
            ],
            axis=0,
        ).astype(BF16)
        high, low = parts(turn(band))
        wyb[v] = jnp.concatenate([high, high, low], axis=1).astype(BF16)

        offset = plan.reach_x + shift_x[v]
        index = (
            lax.broadcasted_iota(jnp.int32, (width, width), 1)
            - lax.broadcasted_iota(jnp.int32, (width, width), 0)
            + offset
        )
        wide = pltpu.roll(slide(taps(kc, v), width, 0), width - offset, 1)
        band = jnp.where((index >= 0) & (index < kc.shape[1]), wide, 0.0)
        for out, matrix in ((wxb, band), (wxf, band.T)):
            high, low = parts(matrix)
            out[v, :width, :width] = high.astype(BF16)
            out[v, :width, width:] = low.astype(BF16)
            out[v, width:, :width] = high.astype(BF16)
            out[v, width:, width:] = jnp.zeros_like(low).astype(BF16)

    for out, begin, count in ((wzu, 0, plan.upright), (wzt, plan.upright, plan.turned)):
        for j in range(3):
            pieces = []
            for v in range(begin, begin + count):
                scale = jnp.where(
                    place_z < zpad,
                    share(0, j, v),
                    jnp.where(place_z < zpad + depth, share(1, j, v), share(2, j, v)),
                )
                pieces.append(kept[v] * scale)
            high, low = parts(jnp.concatenate(pieces, axis=1))
            out[j] = jnp.concatenate([high, high, low], axis=1).astype(BF16)


def bands(plan, place, views_of, shift_x, kd, kr, kc):
    views = plan.upright + plan.turned
    tall = plan.depth + 2 * plan.zpad
    total = plan.rows + plan.side
    shapes = [
        (views * plan.depth, 3 * tall),
        (views, 2 * plan.rows, 2 * total),
        (views, 2 * plan.width, 2 * plan.width),
        (views, 2 * plan.width, 2 * plan.width),
        (views, total, 3 * plan.rows),
        (3, tall, 3 * plan.upright * plan.depth),
        (3, tall, 3 * plan.turned * plan.depth),
    ]
    smem = pl.BlockSpec(memory_space=pltpu.SMEM)
    vmem = pl.BlockSpec(memory_space=pltpu.VMEM)
    return pl.pallas_call(
        functools.partial(bands_kernel, plan),
        out_shape=[jax.ShapeDtypeStruct(x, BF16) for x in shapes],
        in_specs=[smem] * 3 + [vmem] * 3,
        out_specs=[vmem] * len(shapes),
        compiler_params=pltpu.CompilerParams(vmem_limit_bytes=plan.vmem),
        name=plan.name,
    )(place, views_of, shift_x, kd, kr, kc)


def local(
    prior_estimate,
    views_upright,
    views_turned,
    kernel_depth,
    kernel_rows,
    kernel_columns,
    lateral_offsets,
    block_views,
):
    depth, rows, width = prior_estimate.shape
    views = kernel_depth.shape[0]
    reach = (kernel_depth.shape[1] - 1) // 2
    reach_y = (kernel_rows.shape[1] - 1) // 2
    reach_x = (kernel_columns.shape[1] - 1) // 2
    zpad = round_up(reach, 16)
    ypad = round_up(reach_y, 8)
    side = 2 * ypad
    n_xy = lax.axis_size("xy")
    n_gz = lax.axis_size("gz")

    half = views_turned.shape[0]
    per = width // rows
    packed = pack(
        views_turned.reshape(half * depth, views_turned.shape[2], views_turned.shape[3]), n_xy, per
    )
    upright = views_upright.reshape(views - half, depth * rows, width)

    n_up = views - half
    common = dict(
        depth=depth,
        rows=rows,
        side=side,
        reach=reach,
        zpad=zpad,
        width=width,
        upright=n_up,
        turned=half,
        per=per,
        count=n_xy,
        group=16,
        unroll=depth // 16,
    )
    plan = Plan(
        name="bands", vmem=56 << 20, n_gz=n_gz, reach_y=reach_y, reach_x=reach_x, **common
    )
    place = jnp.stack([lax.axis_index("gz"), lax.axis_index("xy")]).astype(jnp.int32)
    wz_f, wy_f, wx_f, wx_b, wy_b, wzb_u, wzb_t = bands(
        plan, place, block_views, lateral_offsets, kernel_depth, kernel_rows, kernel_columns
    )
    flat = lambda x: x.reshape(-1, width)
    cube = lambda x, n: x.reshape(-1, n, width)
    head = ((0, depth - reach), (0, 0), (0, 0))
    tail = ((depth - reach, 0), (0, 0), (0, 0))
    back = dict(wxb=wx_b, wyb=wy_b)
    shared = dict(wzf=wz_f, wyf=wy_f, wxf=wx_f)
    estimate = prior_estimate
    for iteration in range(ITERS):
        from_left, from_right = exchange(
            estimate[:, :ypad], estimate[:, rows - ypad :], "xy"
        )
        if iteration == 0:
            packed, from_left, from_right = lax.optimization_barrier(
                (packed, from_left, from_right)
            )
            received = lax.all_to_all(packed, "xy", split_axis=0, concat_axis=0, tiled=True)
        below, above = exchange(estimate[:reach], estimate[depth - reach :], "gz")
        sides = jnp.concatenate([from_left, from_right], axis=1)
        side_below, side_above = exchange(sides[:reach], sides[depth - reach :], "gz")
        early = ahead(
            Plan(name="ahead", vmem=24 << 20, **common),
            flat(estimate),
            flat(below),
            flat(above),
            wz_f,
        )
        volumes = [flat(x) for x in (sides, side_below, side_above)]
        forth = dict(ahead_c=early.reshape(views, -1, width), volumes=volumes, **shared)
        if iteration == 0:
            *acc, lines_u, blurred = update(
                Plan(
                    name="first",
                    vmem=SPLIT[0] << 20,
                    forward=True,
                    upright_back=True,
                    turned_back=False,
                    **common,
                ),
                obs_u=upright,
                wzb_u=wzb_u,
                **forth,
                **back,
            )
            *parts, lines_t = update(
                Plan(
                    name="second",
                    vmem=SPLIT[1] << 20,
                    forward=False,
                    upright_back=False,
                    turned_back=True,
                    **common,
                ),
                obs_t=received,
                wzb_t=wzb_t,
                blurred=blurred,
                acc=acc,
                **back,
            )
        else:
            *parts, lines_u, lines_t = update(
                Plan(
                    name="both",
                    vmem=SPLIT[2] << 20,
                    forward=True,
                    upright_back=True,
                    turned_back=True,
                    **common,
                ),
                obs_u=upright,
                obs_t=received,
                wzb_u=wzb_u,
                wzb_t=wzb_t,
                **forth,
                **back,
            )
        sc, slo, shi = (cube(x, side) for x in parts)
        cc, clo, chi = (
            cube(x, rows)
            for x in behind(
                Plan(name="behind", vmem=24 << 20, **common), lines_u, lines_t, wzb_u, wzb_t
            )
        )
        s_low, s_high = exchange(slo, shi, "gz")
        c_low, c_high = exchange(clo, chi, "gz")
        sc = sc + jnp.pad(s_low, head) + jnp.pad(s_high, tail)
        from_left, from_right = exchange(sc[:, :ypad], sc[:, ypad:], "xy")
        cc = cc + jnp.pad(c_low, head) + jnp.pad(c_high, tail)
        cc = cc + jnp.pad(from_left, ((0, 0), (0, rows - ypad), (0, 0)))
        cc = cc + jnp.pad(from_right, ((0, 0), (rows - ypad, 0), (0, 0)))
        estimate = estimate * cc
    return estimate


def solution(mesh):
    in_specs = (
        P("gz", "xy", None),
        P(None, "gz", "xy", None),
        P(None, "gz", "xy", None),
        P(),
        P(),
        P(),
        P(),
        P(),
    )
    out_specs = P("gz", "xy", None)
    return jax.shard_map(local, mesh=mesh, in_specs=in_specs, out_specs=out_specs, check_vma=False)
```

```python
import functools

import jax
import jax.numpy as jnp
from jax import lax
from jax.experimental import pallas as pl
from jax.experimental.pallas import tpu as pltpu
from jax.sharding import PartitionSpec as P

ITERS = 2
F32 = jnp.float32
BF16 = jnp.bfloat16
VMEM_LIMIT = 36 * 1024 * 1024
SPLIT = (56, 56, 28)


def round_up(value, unit):
    return -(-value // unit) * unit


def exchange(low, high, axis):
    count = lax.axis_size(axis)
    even = lax.axis_index(axis) % 2 == 0
    rounds = [
        [pair for i in range(begin, count - 1, 2) for pair in ((i, i + 1), (i + 1, i))]
        for begin in (0, 1)
    ]
    a = lax.ppermute(jnp.where(even, high, low), axis, rounds[0])
    b = lax.ppermute(jnp.where(even, low, high), axis, rounds[1])
    return jnp.where(even, b, a), jnp.where(even, a, b)


def halves(value):
    high = value.astype(BF16)
    low = (value - high.astype(F32)).astype(BF16)
    return high, low


def stack(value):
    top, rest = halves(value)
    return jnp.concatenate([top, rest, top], axis=0)


def update_kernel(plan, *refs):
    refs = list(refs)
    take = lambda n: [refs.pop(0) for _ in range(n)]
    depth, rows, side, reach, zpad = plan.depth, plan.rows, plan.side, plan.reach, plan.zpad
    width = plan.width
    total = rows + side
    pitch_c = rows + 2
    pitch_s = side + 2
    pitch_r = depth + 2
    if plan.forward:
        ahead_c, s, slo, shi, wzf, wyf, wxf = take(7)
    if plan.upright_back:
        obs_u, wzb_u = take(2)
    if plan.turned_back:
        obs_t, wzb_t = take(2)
        if not plan.forward:
            (blur_in,) = take(1)
            acc = take(3)
    wxb, wyb = take(2)
    outs = take(3)
    if plan.upright_back:
        (lines_u,) = take(1)
    if plan.turned_back:
        (lines_t,) = take(1)
    else:
        (blur_out,) = take(1)
    if plan.forward:
        (mid,) = take(1)
    (back,) = take(1)
    copies = []
    if plan.turned_back and not plan.forward:
        held = take(3)
        (arrived,) = take(1)
        copies = [
            pltpu.make_async_copy(x, y, arrived.at[i]) for i, (x, y) in enumerate(zip(acc, held))
        ]
        acc = held

        @pl.when(pl.program_id(0) == 0)
        def _():
            for copy in copies:
                copy.start()

    step = pl.program_id(0)
    first = 1 if plan.forward else 0
    n_up = plan.upright if (plan.forward) else 0
    n_all = n_up + plan.turned
    lines = plan.lines
    pitch_z = lines + 8
    group = plan.group

    if plan.forward:

        @pl.when(step == 0)
        def _():
            forward_z(plan, slo, s, shi, side, wzf, pitch_s, mid, n_all * depth)

    def blur_lines(view, i):
        pieces = []
        for j in range(group // 2):
            line = i * group + 2 * j
            both = jnp.concatenate(
                [
                    jnp.concatenate(
                        [
                            ahead_c[0, pl.ds((line + k) * pitch_c, rows), :],
                            mid[pl.ds((view * depth + line + k) * pitch_s, side), :],
                        ],
                        axis=0,
                    )
                    for k in range(2)
                ],
                axis=1,
            )
            top, rest = halves(both)
            result = jnp.dot(
                wyf[0], jnp.concatenate([top, rest], axis=0), preferred_element_type=F32
            )
            result = result[:rows] + result[rows:]
            pieces += [result[:, :width], result[:, width:]]
        top, rest = halves(jnp.concatenate(pieces, axis=0))
        result = jnp.dot(
            jnp.concatenate([top, rest], axis=1), wxf[0], preferred_element_type=F32
        )
        return result[:, :width] + result[:, width:]

    def spread_lines(slot, i, ratio, lines_c):
        top, rest = halves(ratio)
        flat = jnp.dot(jnp.concatenate([top, rest], axis=1), wxb[0], preferred_element_type=F32)
        flat = flat[:, :width] + flat[:, width:]
        for j in range(group // 2):
            both = jnp.concatenate(
                [flat[(2 * j + k) * rows : (2 * j + k + 1) * rows] for k in range(2)], axis=1
            )
            result = jnp.dot(wyb[0], stack(both), preferred_element_type=F32)
            for k in range(2):
                line = i * group + 2 * j + k
                piece = result[:, k * width : (k + 1) * width]
                lines_c[0, pl.ds(line, rows, stride=pitch_r), :] = piece[:rows]
                back[pl.ds(slot * depth + line, side, stride=pitch_z), :] = piece[rows:]

    def turned_lines(i):
        per = plan.per
        blocks = []
        for g in range(group // per):
            at = i * (group // per) + g
            blocks.append(jnp.concatenate([obs_t[k, at] for k in range(plan.count)], axis=0).T)
        return jnp.concatenate(blocks, axis=0)

    size = group * rows
    window = lambda i: pl.ds(pl.multiple_of(i * size, size), size)

    def loop(body):
        def wrapped(i, carry):
            body(i)
            return carry

        lax.fori_loop(0, depth // group, wrapped, 0, unroll=plan.unroll)

    if plan.upright_back:

        @pl.when((step >= first) & (step < first + n_up))
        def _():
            view = step - first

            def body(i):
                spread_lines(view, i, obs_u[0, window(i), :] / blur_lines(view, i), lines_u)

            loop(body)

    @pl.when((step >= first + n_up) & (step < first + n_all))
    def _():
        view = step - first

        def body(i):
            blurred = blur_lines(view, i) if plan.forward else blur_in[0, window(i), :]
            if plan.turned_back:
                spread_lines(view, i, turned_lines(i) / blurred, lines_t)
            else:
                blur_out[0, window(i), :] = blurred

        loop(body)

    @pl.when(step == first + n_all)
    def _():
        for copy in copies:
            copy.wait()
        banks = []
        if plan.upright_back:
            banks.append((wzb_u, 0, plan.upright * depth))
        if plan.turned_back:
            banks.append((wzb_t, n_up * depth, plan.turned * depth))

        def sums(y, region):
            result = None
            for weights, offset, count in banks:
                both = jnp.concatenate(
                    [back[pl.ds((y + j) * pitch_z + offset, count), :] for j in range(2)], axis=1
                )
                term = jnp.dot(weights[region], stack(both), preferred_element_type=F32)
                result = term if result is None else result + term
            return result

        adds = acc if (plan.turned_back and not plan.forward) else [None] * 3
        backward_z(plan, lambda y: sums(y, 0), outs, adds, side, 0, side // 4)
        backward_z(plan, lambda y: sums(y, 2), outs, adds, side, side // 4, side // 2)


def forward_z(plan, low, centre, high, n, weights, pitch, target, count):
    depth, reach = plan.depth, plan.reach
    width = plan.width
    fill = jnp.zeros((plan.zpad - reach, width), F32)

    def column(y):
        return jnp.concatenate(
            [
                low[pl.ds(y, reach, stride=n), :],
                fill,
                centre[pl.ds(y, depth, stride=n), :],
                high[pl.ds(y, reach, stride=n), :],
                fill,
            ],
            axis=0,
        )

    def body(i, carry):
        both = jnp.concatenate([column(2 * i + j) for j in range(2)], axis=1)
        result = jnp.dot(weights[...], stack(both), preferred_element_type=F32)
        for j in range(2):
            target[pl.ds(2 * i + j, count, stride=pitch), :] = result[
                :, j * width : (j + 1) * width
            ]
        return carry

    lax.fori_loop(0, n // 2, body, 0, unroll=8)


def backward_z(plan, sums, targets, adds, n, begin, end, shift=0):
    depth, reach, zpad, width = plan.depth, plan.reach, plan.zpad, plan.width

    def body(i, carry):
        result = sums(2 * i)
        for j in range(2):
            part = result[:, j * width : (j + 1) * width]
            for target, add, low, count in zip(
                targets, adds, (zpad, 0, zpad + depth), (depth, reach, reach)
            ):
                spot = (pl.ds(shift + 2 * i + j, count, stride=n), slice(None))
                piece = part[low : low + count]
                if add is not None:
                    piece = piece + add[spot]
                target[spot] = piece
        return carry

    lax.fori_loop(begin, end, body, 0, unroll=4)


def ahead_kernel(plan, c, clo, chi, wzf, out):
    forward_z(
        plan, clo, c, chi, plan.rows, wzf, plan.rows + 2, out, wzf.shape[0]
    )


def ahead(plan, c, clo, chi, wzf):
    cuts = 2
    whole = lambda x: pl.BlockSpec(x.shape, lambda i: (0, 0), pipeline_mode=pl.Buffered(1))
    lines = wzf.shape[0] * (plan.rows + 2)
    return pl.pallas_call(
        functools.partial(ahead_kernel, plan),
        out_shape=jax.ShapeDtypeStruct((lines, plan.width), F32),
        grid=(cuts,),
        in_specs=[whole(x) for x in (c, clo, chi)]
        + [pl.BlockSpec((wzf.shape[0] // cuts, wzf.shape[1]), lambda i: (i, 0))],
        out_specs=pl.BlockSpec((lines // cuts, plan.width), lambda i: (i, 0)),
        compiler_params=pltpu.CompilerParams(vmem_limit_bytes=plan.vmem),
        cost_estimate=pl.CostEstimate(flops=3 * 10**9, bytes_accessed=8 * 10**6, transcendentals=0),
        name=plan.name,
    )(c, clo, chi, wzf)


def behind_kernel(plan, span, ru, rt, wzu, wzt, cc, clo, chi):
    depth = plan.depth
    begin = pl.program_id(0) * span

    def sums(y):
        result = None
        for lines, weights in ((ru, wzu), (rt, wzt)):
            both = jnp.concatenate(
                [
                    jnp.concatenate(
                        [
                            lines[v, pl.ds((y + j) * (depth + 2), depth), :]
                            for v in range(lines.shape[0])
                        ],
                        axis=0,
                    )
                    for j in range(2)
                ],
                axis=1,
            )
            term = jnp.dot(weights[0], stack(both), preferred_element_type=F32)
            result = term if result is None else result + term
        return result

    backward_z(plan, sums, (cc, clo, chi), [None] * 3, plan.rows, 0, span // 2, begin)


def behind(plan, ru, rt, wzu, wzt):
    span = 8
    pitch = plan.depth + 2
    block = lambda x: pl.BlockSpec((x.shape[0], span * pitch, plan.width), lambda i: (0, i, 0))
    weights = lambda x: pl.BlockSpec((1,) + x.shape[1:], lambda i: (1, 0, 0))
    shapes = [
        jax.ShapeDtypeStruct((count * plan.rows, plan.width), F32)
        for count in (plan.depth, plan.reach, plan.reach)
    ]
    return pl.pallas_call(
        functools.partial(behind_kernel, plan, span),
        out_shape=shapes,
        grid=(plan.rows // span,),
        in_specs=[block(ru), block(rt), weights(wzu), weights(wzt)],
        out_specs=[
            pl.BlockSpec(x.shape, lambda i: (0, 0), pipeline_mode=pl.Buffered(1)) for x in shapes
        ],
        compiler_params=pltpu.CompilerParams(vmem_limit_bytes=plan.vmem),
        cost_estimate=pl.CostEstimate(flops=3 * 10**9, bytes_accessed=8 * 10**6, transcendentals=0),
        name=plan.name,
    )(ru, rt, wzu, wzt)


class Plan:
    def __init__(self, **fields):
        self.__dict__.update(fields)


def update(plan, **a):
    first = 1 if plan.forward else 0
    n_up = plan.upright if plan.forward else 0
    n_all = n_up + plan.turned
    used = (plan.upright if plan.upright_back else 0) + (plan.turned if plan.turned_back else 0)
    plan.lines = used * plan.depth
    shift = plan.upright - n_up
    once = pl.Buffered(1)

    def whole(x):
        return pl.BlockSpec(x.shape, lambda i: (0,) * len(x.shape), pipeline_mode=once)

    def per_view(x, start, count, offset=0):
        return pl.BlockSpec(
            (1,) + x.shape[1:],
            lambda i: (jnp.clip(i - start, 0, count - 1) + offset,) + (0,) * (len(x.shape) - 1),
        )

    args, specs = [], []

    def give(x, spec):
        args.append(x)
        specs.append(spec)

    if plan.forward:
        give(a["ahead_c"], per_view(a["ahead_c"], first, n_all))
        for x in a["volumes"]:
            give(x, whole(x))
        give(a["wzf"], whole(a["wzf"]))
        give(a["wyf"], per_view(a["wyf"], first, n_all))
        give(a["wxf"], per_view(a["wxf"], first, n_all))
    if plan.upright_back:
        give(a["obs_u"], per_view(a["obs_u"], first, plan.upright))
        give(a["wzb_u"], whole(a["wzb_u"]))
    if plan.turned_back:
        x = a["obs_t"]
        begin = first + n_up
        give(
            x,
            pl.BlockSpec(
                (x.shape[0], x.shape[1] // plan.turned) + x.shape[2:],
                lambda i: (0, jnp.clip(i - begin, 0, plan.turned - 1), 0, 0),
            ),
        )
        give(a["wzb_t"], whole(a["wzb_t"]))
        if not plan.forward:
            give(a["blurred"], per_view(a["blurred"], begin, plan.turned))
            for x in a["acc"]:
                give(x, pl.BlockSpec(memory_space=pl.ANY))
    backs = plan.upright if not plan.turned_back else n_all
    give(a["wxb"], per_view(a["wxb"], first, backs, shift))
    give(a["wyb"], per_view(a["wyb"], first, backs, shift))

    shapes = [
        jax.ShapeDtypeStruct((count * n, plan.width), F32)
        for n in (plan.side,)
        for count in (plan.depth, plan.reach, plan.reach)
    ]
    out_specs = [whole(x) for x in shapes]
    for used, begin, count in (
        (plan.upright_back, first, plan.upright),
        (plan.turned_back, first + n_up, plan.turned),
    ):
        if used:
            x = jax.ShapeDtypeStruct((count, plan.rows * (plan.depth + 2), plan.width), F32)
            shapes.append(x)
            out_specs.append(per_view(x, begin, count))
    if not plan.turned_back:
        x = jax.ShapeDtypeStruct((plan.turned, plan.depth * plan.rows, plan.width), F32)
        shapes.append(x)
        out_specs.append(per_view(x, first + n_up, plan.turned))
    scratch = []
    if plan.forward:
        scratch.append(pltpu.VMEM((n_all * plan.depth * (plan.side + 2), plan.width), F32))
    scratch.append(pltpu.VMEM((plan.side * (plan.lines + 8), plan.width), F32))
    if plan.turned_back and not plan.forward:
        scratch += [pltpu.VMEM(x.shape, F32) for x in a["acc"]]
        scratch.append(pltpu.SemaphoreType.DMA((len(a["acc"]),)))
    return pl.pallas_call(
        functools.partial(update_kernel, plan),
        out_shape=shapes,
        grid=(first + n_all + 1,),
        in_specs=specs,
        out_specs=out_specs,
        scratch_shapes=scratch,
        compiler_params=pltpu.CompilerParams(vmem_limit_bytes=plan.vmem),
        cost_estimate=pl.CostEstimate(
            flops=10**10, bytes_accessed=12 * 10**6, transcendentals=0
        ),
        name=plan.name,
    )(*args)


def pack_kernel(count, per, x, out):
    rows = x.shape[-1] // count
    for g in range(x.shape[0] // per):
        for d in range(count):
            out[d, g] = jnp.concatenate(
                [x[g * per + j, :, d * rows : (d + 1) * rows] for j in range(per)], axis=1
            )


def pack(turned, count, per):
    planes, xl, yf = turned.shape
    block = 48 if planes % 48 == 0 else per
    return pl.pallas_call(
        functools.partial(pack_kernel, count, per),
        out_shape=jax.ShapeDtypeStruct((count, planes // per, xl, per * (yf // count)), F32),
        grid=(planes // block,),
        in_specs=[pl.BlockSpec((block, xl, yf), lambda i: (i, 0, 0))],
        out_specs=pl.BlockSpec(
            (count, block // per, xl, per * (yf // count)), lambda i: (0, i, 0, 0)
        ),
        compiler_params=pltpu.CompilerParams(vmem_limit_bytes=VMEM_LIMIT),
        name="pack",
    )(turned)


def bands_kernel(plan, place, views_of, shift_x, kd, kr, kc, wzf, wyf, wxf, wxb, wyb, wzu, wzt):
    depth, rows, side, reach, zpad = plan.depth, plan.rows, plan.side, plan.reach, plan.zpad
    width = plan.width
    ypad = side // 2
    gap = zpad - reach
    active = views_of.shape[1]

    def taps(ref, v):
        row = ref[v : v + 1, :]
        row = row / jnp.sum(row, axis=1, keepdims=True)
        return jnp.concatenate([row, jnp.zeros((1, width - row.shape[1]), F32)], axis=1)

    def slide(row, height, amount):
        base = jnp.broadcast_to(row, (height, width))
        return pltpu.roll(base, amount, 1, stride=1, stride_axis=0)

    def parts(matrix):
        high = matrix.astype(BF16).astype(F32)
        return high, matrix - high

    def turn(matrix):
        rows_in, cols_in = matrix.shape
        square = jnp.concatenate([matrix, jnp.zeros((width - rows_in, cols_in), F32)], axis=0)
        square = jnp.concatenate([square, jnp.zeros((width, width - cols_in), F32)], axis=1)
        return square.T[:cols_in, :rows_in]

    def share(i, j, v):
        z = jnp.clip(place[0] + i - 1, 0, plan.n_gz - 1)
        y = jnp.clip(place[1] + j - 1, 0, plan.count - 1)
        found = jnp.int32(0)
        for k in range(active):
            found = found + (views_of[z * plan.count + y, k] == v).astype(jnp.int32)
        return found.astype(F32) / active

    place_z = lax.broadcasted_iota(jnp.int32, (depth + 2 * zpad, depth), 0)
    kept = []
    for v in range(plan.upright + plan.turned):
        wide = slide(taps(kd, v), depth, 0)
        zeros = jnp.zeros((depth, gap), F32)
        band = jnp.concatenate(
            [
                wide[:, :reach],
                zeros,
                wide[:, reach : reach + depth],
                wide[:, reach + depth : 2 * reach + depth],
                zeros,
            ],
            axis=1,
        )
        high, low = parts(band)
        wzf[v * depth : (v + 1) * depth, :] = jnp.concatenate([high, high, low], axis=1).astype(
            BF16
        )
        kept.append(turn(band))

        wide = slide(taps(kr, v), rows, ypad - plan.reach_y)
        band = jnp.concatenate(
            [wide[:, ypad : ypad + rows], wide[:, :ypad], wide[:, ypad + rows : 2 * ypad + rows]],
            axis=1,
        )
        high, low = parts(band)
        wyf[v] = jnp.concatenate(
            [
                jnp.concatenate([high, high], axis=1),
                jnp.concatenate([low, jnp.zeros_like(low)], axis=1),
            ],
            axis=0,
        ).astype(BF16)
        high, low = parts(turn(band))
        wyb[v] = jnp.concatenate([high, high, low], axis=1).astype(BF16)

        offset = plan.reach_x + shift_x[v]
        index = (
            lax.broadcasted_iota(jnp.int32, (width, width), 1)
            - lax.broadcasted_iota(jnp.int32, (width, width), 0)
            + offset
        )
        wide = pltpu.roll(slide(taps(kc, v), width, 0), width - offset, 1)
        band = jnp.where((index >= 0) & (index < kc.shape[1]), wide, 0.0)
        for out, matrix in ((wxb, band), (wxf, band.T)):
            high, low = parts(matrix)
            out[v, :width, :width] = high.astype(BF16)
            out[v, :width, width:] = low.astype(BF16)
            out[v, width:, :width] = high.astype(BF16)
            out[v, width:, width:] = jnp.zeros_like(low).astype(BF16)

    for out, begin, count in ((wzu, 0, plan.upright), (wzt, plan.upright, plan.turned)):
        for j in range(3):
            pieces = []
            for v in range(begin, begin + count):
                scale = jnp.where(
                    place_z < zpad,
                    share(0, j, v),
                    jnp.where(place_z < zpad + depth, share(1, j, v), share(2, j, v)),
                )
                pieces.append(kept[v] * scale)
            high, low = parts(jnp.concatenate(pieces, axis=1))
            out[j] = jnp.concatenate([high, high, low], axis=1).astype(BF16)


def bands(plan, place, views_of, shift_x, kd, kr, kc):
    views = plan.upright + plan.turned
    tall = plan.depth + 2 * plan.zpad
    total = plan.rows + plan.side
    shapes = [
        (views * plan.depth, 3 * tall),
        (views, 2 * plan.rows, 2 * total),
        (views, 2 * plan.width, 2 * plan.width),
        (views, 2 * plan.width, 2 * plan.width),
        (views, total, 3 * plan.rows),
        (3, tall, 3 * plan.upright * plan.depth),
        (3, tall, 3 * plan.turned * plan.depth),
    ]
    smem = pl.BlockSpec(memory_space=pltpu.SMEM)
    vmem = pl.BlockSpec(memory_space=pltpu.VMEM)
    return pl.pallas_call(
        functools.partial(bands_kernel, plan),
        out_shape=[jax.ShapeDtypeStruct(x, BF16) for x in shapes],
        in_specs=[smem] * 3 + [vmem] * 3,
        out_specs=[vmem] * len(shapes),
        compiler_params=pltpu.CompilerParams(vmem_limit_bytes=plan.vmem),
        name=plan.name,
    )(place, views_of, shift_x, kd, kr, kc)


def local(
    prior_estimate,
    views_upright,
    views_turned,
    kernel_depth,
    kernel_rows,
    kernel_columns,
    lateral_offsets,
    block_views,
):
    depth, rows, width = prior_estimate.shape
    views = kernel_depth.shape[0]
    reach = (kernel_depth.shape[1] - 1) // 2
    reach_y = (kernel_rows.shape[1] - 1) // 2
    reach_x = (kernel_columns.shape[1] - 1) // 2
    zpad = round_up(reach, 16)
    ypad = round_up(reach_y, 8)
    side = 2 * ypad
    n_xy = lax.axis_size("xy")
    n_gz = lax.axis_size("gz")

    half = views_turned.shape[0]
    per = width // rows
    packed = pack(
        views_turned.reshape(half * depth, views_turned.shape[2], views_turned.shape[3]), n_xy, per
    )
    upright = views_upright.reshape(views - half, depth * rows, width)

    n_up = views - half
    common = dict(
        depth=depth,
        rows=rows,
        side=side,
        reach=reach,
        zpad=zpad,
        width=width,
        upright=n_up,
        turned=half,
        per=per,
        count=n_xy,
        group=16,
        unroll=depth // 16,
    )
    plan = Plan(
        name="bands", vmem=56 << 20, n_gz=n_gz, reach_y=reach_y, reach_x=reach_x, **common
    )
    place = jnp.stack([lax.axis_index("gz"), lax.axis_index("xy")]).astype(jnp.int32)
    wz_f, wy_f, wx_f, wx_b, wy_b, wzb_u, wzb_t = bands(
        plan, place, block_views, lateral_offsets, kernel_depth, kernel_rows, kernel_columns
    )
    flat = lambda x: x.reshape(-1, width)
    cube = lambda x, n: x.reshape(-1, n, width)
    head = ((0, depth - reach), (0, 0), (0, 0))
    tail = ((depth - reach, 0), (0, 0), (0, 0))
    back = dict(wxb=wx_b, wyb=wy_b)
    shared = dict(wzf=wz_f, wyf=wy_f, wxf=wx_f)
    estimate = prior_estimate
    for iteration in range(ITERS):
        from_left, from_right = exchange(
            estimate[:, :ypad], estimate[:, rows - ypad :], "xy"
        )
        if iteration == 0:
            packed, from_left, from_right = lax.optimization_barrier(
                (packed, from_left, from_right)
            )
            received = lax.all_to_all(packed, "xy", split_axis=0, concat_axis=0, tiled=True)
        below, above = exchange(estimate[:reach], estimate[depth - reach :], "gz")
        sides = jnp.concatenate([from_left, from_right], axis=1)
        side_below, side_above = exchange(sides[:reach], sides[depth - reach :], "gz")
        early = ahead(
            Plan(name="ahead", vmem=24 << 20, **common),
            flat(estimate),
            flat(below),
            flat(above),
            wz_f,
        )
        volumes = [flat(x) for x in (sides, side_below, side_above)]
        forth = dict(ahead_c=early.reshape(views, -1, width), volumes=volumes, **shared)
        if iteration == 0:
            *acc, lines_u, blurred = update(
                Plan(
                    name="first",
                    vmem=SPLIT[0] << 20,
                    forward=True,
                    upright_back=True,
                    turned_back=False,
                    **common,
                ),
                obs_u=upright,
                wzb_u=wzb_u,
                **forth,
                **back,
            )
            *parts, lines_t = update(
                Plan(
                    name="second",
                    vmem=SPLIT[1] << 20,
                    forward=False,
                    upright_back=False,
                    turned_back=True,
                    **common,
                ),
                obs_t=received,
                wzb_t=wzb_t,
                blurred=blurred,
                acc=acc,
                **back,
            )
        else:
            *parts, lines_u, lines_t = update(
                Plan(
                    name="both",
                    vmem=SPLIT[2] << 20,
                    forward=True,
                    upright_back=True,
                    turned_back=True,
                    **common,
                ),
                obs_u=upright,
                obs_t=received,
                wzb_u=wzb_u,
                wzb_t=wzb_t,
                **forth,
                **back,
            )
        sc, slo, shi = (cube(x, side) for x in parts)
        cc, clo, chi = (
            cube(x, rows)
            for x in behind(
                Plan(name="behind", vmem=24 << 20, **common), lines_u, lines_t, wzb_u, wzb_t
            )
        )
        s_low, s_high = exchange(slo, shi, "gz")
        c_low, c_high = exchange(clo, chi, "gz")
        sc = sc + jnp.pad(s_low, head) + jnp.pad(s_high, tail)
        from_left, from_right = exchange(sc[:, :ypad], sc[:, ypad:], "xy")
        cc = cc + jnp.pad(c_low, head) + jnp.pad(c_high, tail)
        cc = cc + jnp.pad(from_left, ((0, 0), (0, rows - ypad), (0, 0)))
        cc = cc + jnp.pad(from_right, ((0, 0), (rows - ypad, 0), (0, 0)))
        estimate = estimate * cc
    return estimate


def solution(mesh):
    in_specs = (
        P("gz", "xy", None),
        P(None, "gz", "xy", None),
        P(None, "gz", "xy", None),
        P(),
        P(),
        P(),
        P(),
        P(),
    )
    out_specs = P("gz", "xy", None)
    return jax.shard_map(local, mesh=mesh, in_specs=in_specs, out_specs=out_specs, check_vma=False)
```
